32 devices in a mesh: seq: 32 (over z, y, x, core).
Axes of the slice: x: 2, y: 2, z: 4, core: 2. Of those that a mesh axis runs over, the one named last changes fastest.
Arguments:
- tokens: bfloat16 [16384, 1024], P('seq'), may hold values from -128 to 128, as said below
- w_query: bfloat16 [1024, 1024], replicated, may hold values from -0.1875 to 0.1875
- w_key: bfloat16 [1024, 256], replicated, may hold values from -0.1875 to 0.1875
- w_value: bfloat16 [1024, 256], replicated, may hold values from -0.1875 to 0.1875
- w_out: bfloat16 [1024, 1024], replicated, may hold values from -0.1875 to 0.1875
Outputs:
- attended: bfloat16 [16384, 1024], P('seq')
The draws below stay inside these ranges and needn't reach their ends.
Inputs may be any that keep to these rules, and one draw needn't show every extreme that they name: `tokens`: Real-valued activations.
All inputs are finite; a program needn't handle non-finite values.
Results may differ from the reference program's by a relative error of at most 0.007.
The reference program's roundings to bfloat16 on the way (of `queries`, `key_rows`, `value_rows`, `middle`, `coarse`, `probabilities` and `mixed`) count: a program that leaves them out, or rounds other values in their place, can miss the bound.
Values may be sent and summed in bfloat16 or wider, within the bound.
No kernel may reach another device: no remote copies, remote signals or barrier semaphores. Data moves between devices by JAX's collectives and lax.ppermute only.
A program may use at most 128 MiB of HBM per device.

```python
import math
import jax
import jax.numpy as jnp
from jax import lax

D = 1024
HEADS = 16
KV_HEADS = 4
HEAD_DIM = 64
BLOCK = 256
POOL = 16
GROUP = 16
TOK_DEV = 512
SEQ = 16384


def draw_tokens(key, part):
    block_total = SEQ // BLOCK
    run_total = SEQ // POOL
    block_vectors = jnp.clip(jax.random.normal(jax.random.fold_in(key, 21), (block_total, D), jnp.float32), -6.0, 6.0)
    run_vectors = jnp.clip(jax.random.normal(jax.random.fold_in(key, 22), (run_total, D), jnp.float32), -6.0, 6.0)
    noise_rows = jnp.clip(jax.random.normal(jax.random.fold_in(key, 11), (SEQ, D), jnp.float32), -6.0, 6.0)
    sample_rows = 0.45 * noise_rows.reshape(run_total, POOL, D) + 0.4 * run_vectors[:, None, :]
    sample_rows = sample_rows.reshape(block_total, BLOCK, D) + 0.8 * block_vectors[:, None, :]
    sample_rows = 1.6 * sample_rows
    sample_rows = jnp.clip(sample_rows.reshape(SEQ, D), -128.0, 128.0)
    return sample_rows.astype(jnp.bfloat16)


def centred(rng, shape, scale, bound, held_as=jnp.bfloat16):
    return jnp.clip(scale * jax.random.normal(rng, shape, jnp.float32), -bound, bound).astype(held_as)


def setup_inputs(seed: int = 0) -> dict:
    seeds = jax.random.split(jax.random.key(seed), 6)
    tokens = draw_tokens(jax.random.fold_in(seeds[5], 71), 0)
    w_query = centred(seeds[1], (D, HEADS * HEAD_DIM), D ** -0.5, 0.1875)
    w_key = centred(seeds[2], (D, KV_HEADS * HEAD_DIM), D ** -0.5, 0.1875)
    w_value = centred(seeds[3], (D, KV_HEADS * HEAD_DIM), D ** -0.5, 0.1875)
    w_out = centred(seeds[4], (HEADS * HEAD_DIM, D), (HEADS * HEAD_DIM) ** -0.5, 0.1875)
    return dict(tokens=tokens, w_query=w_query, w_key=w_key, w_value=w_value, w_out=w_out)


def pool_rows(source, factor):
    width = source.shape[-1]
    grouped = source.astype(jnp.float32).reshape(-1, factor, width)
    return lax.optimization_barrier(jnp.mean(grouped, axis=1)).astype(jnp.bfloat16)

def usable_rows(block_index, my_group, all_blocks, group_tokens, group_summaries):
    near = block_index - 1 + jnp.arange(3 * BLOCK, dtype=jnp.int32) // BLOCK
    near_usable = (near >= 0) & (near < all_blocks)
    middle_blocks = (my_group * group_summaries + jnp.arange(group_summaries, dtype=jnp.int32)) * POOL // BLOCK
    middle_usable = jnp.abs(middle_blocks - block_index) > 1
    coarse_blocks = jnp.arange(all_blocks, dtype=jnp.int32)
    coarse_usable = (coarse_blocks * BLOCK // group_tokens != my_group) & (jnp.abs(coarse_blocks - block_index) > 1)
    return jnp.concatenate([near_usable, middle_usable, coarse_usable])

def attend_block(queries, pair_rows, usable):
    span_rows = pair_rows.shape[0]
    key_width = KV_HEADS * HEAD_DIM
    key_rows = pair_rows[:, :key_width].reshape(span_rows, KV_HEADS, HEAD_DIM).astype(jnp.float32)
    value_rows = pair_rows[:, key_width:].reshape(span_rows, KV_HEADS, HEAD_DIM).astype(jnp.float32)
    shaped = queries.reshape(-1, KV_HEADS, HEADS // KV_HEADS, HEAD_DIM).astype(jnp.float32)
    scores = jnp.einsum('qkgd,lkd->kgql', shaped, key_rows) * (1.0 / math.sqrt(HEAD_DIM))
    scores = jnp.where(usable, scores, -1e+30)
    highest = lax.optimization_barrier(jnp.max(scores, axis=-1, keepdims=True))
    weights = jnp.where(usable, jnp.exp(scores - highest), 0.0)
    totals = lax.optimization_barrier(jnp.sum(weights, axis=-1))
    probabilities = weights.astype(jnp.bfloat16)
    weighted = jnp.einsum('kgql,lkd->qkgd', probabilities.astype(jnp.float32), value_rows)
    weighted = weighted / jnp.transpose(totals, (2, 0, 1))[..., None]
    return weighted.reshape(queries.shape[0], HEADS * HEAD_DIM).astype(jnp.bfloat16)

def reference(tokens, w_query, w_key, w_value, w_out):
    queries = jnp.dot(tokens, w_query, preferred_element_type=jnp.float32).astype(jnp.bfloat16)
    key_rows = jnp.dot(tokens, w_key, preferred_element_type=jnp.float32).astype(jnp.bfloat16)
    value_rows = jnp.dot(tokens, w_value, preferred_element_type=jnp.float32).astype(jnp.bfloat16)
    pair_rows = jnp.concatenate([key_rows, value_rows], axis=1)
    middle = pool_rows(pair_rows, POOL)
    coarse = pool_rows(pair_rows, BLOCK)
    all_blocks = SEQ // BLOCK
    group_tokens = GROUP * TOK_DEV
    group_summaries = group_tokens // POOL
    padded = jnp.pad(pair_rows, ((BLOCK, BLOCK), (0, 0)))

    def per_block(block_index):
        my_group = block_index * BLOCK // group_tokens
        near_rows = lax.dynamic_slice_in_dim(padded, (block_index * BLOCK).astype(jnp.int32), 3 * BLOCK, 0)
        group_mid = lax.dynamic_slice_in_dim(middle, (my_group * group_summaries).astype(jnp.int32), group_summaries, 0)
        block_queries = lax.dynamic_slice_in_dim(queries, (block_index * BLOCK).astype(jnp.int32), BLOCK, 0)
        gathered = jnp.concatenate([near_rows, group_mid, coarse], axis=0)
        usable = usable_rows(block_index, my_group, all_blocks, group_tokens, group_summaries)
        return attend_block(block_queries, gathered, usable)
    mixed = lax.map(per_block, jnp.arange(all_blocks, dtype=jnp.int32)).reshape(SEQ, HEADS * HEAD_DIM)
    return jnp.dot(mixed, w_out, preferred_element_type=jnp.float32).astype(jnp.bfloat16)
```

```python
import functools
import math

import jax
import jax.numpy as jnp
from jax import lax
from jax.experimental import pallas as pl
from jax.experimental.pallas import tpu as pltpu
from jax.sharding import PartitionSpec as P

HEADS = 16
KV_HEADS = 4
HEAD_DIM = 64
BLOCK = 256
POOL = 16
GROUP = 16
SHARE = HEADS // KV_HEADS
WIDE = 128
VROWS = 80
BF16 = jnp.bfloat16
F32 = jnp.float32
NT = (((1,), (1,)), ((), ()))
TN = (((0,), (0,)), ((), ()))
MASKED = -1e30
HOPS = (2, 4, 8, 1)
VMEM = pl.BlockSpec(memory_space=pltpu.VMEM)


def swap(rows, apart):
    count = lax.axis_size("seq")
    return lax.ppermute(rows, "seq", [(i, i ^ apart) for i in range(count)])


def place(slot):
    return sum(hop for bit, hop in enumerate(HOPS) if slot >> bit & 1)


def project_pair(tokens_ref, wk_ref, wv_ref, pair_ref, mid_ref, coarse_ref):
    tokens = tokens_ref[...]
    rows = tokens.shape[0]
    width = wk_ref.shape[1]
    for part, weight in enumerate((wk_ref, wv_ref)):
        at = slice(part * width, (part + 1) * width)
        held = jnp.dot(tokens, weight[...], preferred_element_type=F32).astype(BF16)
        pair_ref[:, at] = held
        for factor, target in ((POOL, mid_ref), (BLOCK, coarse_ref)):
            kept = target.shape[0]
            first = lax.broadcasted_iota(jnp.int32, (kept, rows), 0) * factor
            inside = lax.broadcasted_iota(jnp.int32, (kept, rows), 1) - first
            share = jnp.where((inside >= 0) & (inside < factor), 1.0 / factor, 0.0)
            mean = jnp.dot(share.astype(BF16), held, preferred_element_type=F32)
            target[:, at] = mean.astype(BF16)


def put_keys(keys_ref, rows, at, count, bias):
    lane = lax.broadcasted_iota(jnp.int32, (count, HEAD_DIM), 1)
    extra = jnp.where(lane == 0, 0.0 if bias is None else bias, 0.0).astype(BF16)
    for head in range(KV_HEADS):
        keys_ref[head, at : at + count, :HEAD_DIM] = rows[:, head * HEAD_DIM : (head + 1) * HEAD_DIM]
        keys_ref[head, at : at + count, HEAD_DIM:] = extra


def put_values(values_ref, rows):
    width = KV_HEADS * HEAD_DIM
    count = rows.shape[0]
    tall = KV_HEADS * VROWS
    row = lax.broadcasted_iota(jnp.int32, (tall, width), 0)
    column = lax.broadcasted_iota(jnp.int32, (tall, width), 1)
    head, inner = column // HEAD_DIM, column % HEAD_DIM
    pick = jnp.where(row == head * VROWS + inner, 1.0, 0.0).astype(BF16)
    turned = lax.dot_general(pick, rows, NT, preferred_element_type=F32)
    counting = lax.broadcasted_iota(jnp.int32, (tall, count), 0) % VROWS == HEAD_DIM
    values_ref[...] = jnp.where(counting, 1.0, turned).astype(BF16).reshape(KV_HEADS, VROWS, count)


def run_units(units, scores, finish, values, even, odd):
    def first(unit, buffers):
        held, top = buffers
        x, floor = scores(unit)
        held[...] = x
        highest = jnp.max(x, axis=0, keepdims=True)
        top[...] = highest if floor is None else jnp.maximum(highest, floor)

    def second(unit, buffers):
        held, top = buffers
        highest = top[...]
        weights = jnp.exp(held[...] - highest).astype(BF16)
        finish(unit, highest, jnp.dot(values(unit), weights, preferred_element_type=F32))

    first(0, even)

    def step(i, carry):
        first(2 * i + 1, odd)
        second(2 * i, even)
        first(2 * i + 2, even)
        second(2 * i + 1, odd)
        return carry

    lax.fori_loop(0, units // 2 - 1, step, 0)
    first(units - 1, odd)
    second(units - 2, even)
    second(units - 1, odd)


def early(tokens_ref, wq_ref, pair_ref, q_ref, acc_ref, top_ref, keys_ref, values_ref, sa, ta, sb, tb):
    rows = tokens_ref.shape[0]
    blocks = rows // BLOCK
    width = KV_HEADS * HEAD_DIM
    put_keys(keys_ref, pair_ref[:, :width], 0, rows, None)
    put_values(values_ref, pair_ref[:, width:])
    lane = lax.broadcasted_iota(jnp.int32, (rows, HEAD_DIM), 1)
    extra = jnp.where(lane == 0, 1.0, 0.0).astype(BF16)
    for group in range(KV_HEADS):
        span = SHARE * HEAD_DIM
        part = jnp.dot(tokens_ref[...], wq_ref[:, group * span : (group + 1) * span], preferred_element_type=F32)
        part = part.astype(BF16) * (1.0 / math.sqrt(HEAD_DIM))
        for head in range(SHARE):
            for block in range(blocks):
                at = slice(head * BLOCK, (head + 1) * BLOCK)
                piece = part[block * BLOCK : (block + 1) * BLOCK, head * HEAD_DIM : (head + 1) * HEAD_DIM]
                q_ref[group * blocks + block, at, :HEAD_DIM] = piece
                q_ref[group * blocks + block, at, HEAD_DIM:] = extra[:BLOCK]

    def scores(unit):
        return lax.dot_general(keys_ref[unit // blocks], q_ref[unit], NT, preferred_element_type=F32), None

    def finish(unit, highest, total):
        acc_ref[unit] = total
        top_ref[unit] = highest

    run_units(KV_HEADS * blocks, scores, finish, lambda unit: values_ref[unit // blocks], (sa, ta), (sb, tb))


def late(q_ref, acc_ref, top_ref, prev_ref, next_ref, x_ref, y_ref, z_ref, c_ref, far_ref, wout_ref,
         out_ref, keys_ref, values_ref, mixed_ref, sa, ta, sb, tb):
    blocks = keys_ref.shape[0]
    width = KV_HEADS * HEAD_DIM
    me = lax.axis_index("seq")
    devices = lax.axis_size("seq")
    groups = devices // GROUP
    runs = BLOCK // POOL
    per_device = runs * blocks
    far_rows = far_ref.shape[0]
    pieces = [(far_ref, far_rows), (x_ref, per_device), (y_ref, 2 * per_device), (z_ref, 4 * per_device), (c_ref, 8 * per_device)]
    spread = blocks * (groups - 1)
    row = lax.broadcasted_iota(jnp.int32, (far_rows, HEAD_DIM), 0)
    slot = row // spread
    owner = jnp.zeros_like(row)
    for bit, hop in enumerate(HOPS):
        owner = owner + (slot // 2**bit % 2) * hop
    other = (row % spread) // blocks + 1
    far_block = (((me // GROUP) ^ other) * GROUP + ((me % GROUP) ^ owner)) * blocks + row % blocks
    mid_count = (GROUP - 1) * per_device
    row = lax.broadcasted_iota(jnp.int32, (mid_count, HEAD_DIM), 0) + per_device
    slot = row // per_device
    owner = jnp.zeros_like(row)
    for bit, hop in enumerate(HOPS):
        owner = owner + (slot // 2**bit % 2) * hop
    mid_block = (me ^ owner) * blocks + row % per_device // runs
    for block in range(blocks):
        index = me * blocks + block
        if block == 0:
            near_ref, exists = prev_ref, me > 0
        else:
            near_ref, exists = next_ref, me < devices - 1
        keys = keys_ref.at[block]
        put_keys(keys, near_ref[:, :width], 0, BLOCK, jnp.where(exists, 0.0, MASKED))
        put_keys(keys, far_ref[:, :width], BLOCK, far_rows, jnp.where(jnp.abs(far_block - index) > 1, 0.0, MASKED))
        bias = jnp.where(jnp.abs(mid_block - index) > 1, 0.0, MASKED)
        at = 0
        for piece, count in pieces[1:]:
            put_keys(keys, piece[:count, :width], BLOCK + far_rows + at, count, bias[at : at + count])
            at += count
        gathered = jnp.concatenate([near_ref[:, width:]] + [piece[:count, width:] for piece, count in pieces], axis=0)
        put_values(values_ref.at[block], gathered)

    def scores(unit):
        x = lax.dot_general(keys_ref[unit % blocks, unit // blocks], q_ref[unit], NT, preferred_element_type=F32)
        return x, top_ref[unit]

    def finish(unit, highest, total):
        total = total + acc_ref[unit] * jnp.exp(top_ref[unit] - highest)
        share = total[:HEAD_DIM] / total[HEAD_DIM : HEAD_DIM + 1]
        share = share.astype(BF16)
        for head in range(SHARE):
            at = pl.multiple_of((unit // blocks * SHARE + head) * HEAD_DIM, HEAD_DIM)
            mixed_ref[unit % blocks, pl.ds(at, HEAD_DIM), :] = share[:, head * BLOCK : (head + 1) * BLOCK]

    run_units(KV_HEADS * blocks, scores, finish, lambda unit: values_ref[unit % blocks, unit // blocks], (sa, ta), (sb, tb))
    for block in range(blocks):
        done = lax.dot_general(mixed_ref[block], wout_ref[...], TN, preferred_element_type=F32)
        out_ref[block * BLOCK : (block + 1) * BLOCK] = done.astype(BF16)


def body(tokens, w_query, w_key, w_value, w_out):
    devices = lax.axis_size("seq")
    me = lax.axis_index("seq")
    rows, model = tokens.shape
    blocks = rows // BLOCK
    pair_width = 2 * KV_HEADS * HEAD_DIM
    units = KV_HEADS * blocks
    stack = SHARE * BLOCK
    shape = jax.ShapeDtypeStruct
    params = lambda mib: pltpu.CompilerParams(vmem_limit_bytes=mib * 2**20)
    pair, mid, coarse = pl.pallas_call(
        project_pair,
        out_shape=[shape((rows, pair_width), BF16), shape((rows // POOL, pair_width), BF16), shape((blocks, pair_width), BF16)],
        in_specs=[VMEM] * 3,
        out_specs=[VMEM] * 3,
        compiler_params=params(16),
        cost_estimate=pl.CostEstimate(flops=2 * rows * model * pair_width, bytes_accessed=3 * 2**20, transcendentals=0),
        name="pair",
    )(tokens, w_key, w_value)

    groups = devices // GROUP
    before = lax.ppermute(pair[-BLOCK:], "seq", [(i, i + 1) for i in range(devices - 1)])
    after = lax.ppermute(pair[:BLOCK], "seq", [(i + 1, i) for i in range(devices - 1)])
    if groups == 2:
        spread = jnp.concatenate([swap(coarse, GROUP), swap(coarse, GROUP ^ HOPS[0])], axis=0)
    else:
        spread = coarse
        level = GROUP
        while level < devices:
            spread = jnp.concatenate([spread, swap(spread, level)], axis=0)
            level *= 2
        spread = spread[blocks:]
        spread = jnp.concatenate([spread, swap(spread, HOPS[0])], axis=0)
    held = mid
    arrived = swap(mid, HOPS[0])
    received = [arrived]
    for hop in HOPS[1:]:
        held = jnp.concatenate([held, arrived], axis=0)
        both = swap(jnp.concatenate([held, spread], axis=0), hop)
        arrived = both[: held.shape[0]]
        received.append(both)
        spread = jnp.concatenate([spread, both[held.shape[0] :]], axis=0)

    s_early = [pltpu.VMEM((rows, stack), F32), pltpu.VMEM((1, stack), F32)]
    q, acc, top = pl.pallas_call(
        early,
        out_shape=[shape((units, stack, WIDE), BF16), shape((units, VROWS, stack), F32), shape((units, 1, stack), F32)],
        in_specs=[VMEM] * 3,
        out_specs=[VMEM] * 3,
        scratch_shapes=[pltpu.VMEM((KV_HEADS, rows, WIDE), BF16), pltpu.VMEM((KV_HEADS, VROWS, rows), BF16)] + s_early + s_early,
        compiler_params=params(32),
        cost_estimate=pl.CostEstimate(flops=8 * 10**9, bytes_accessed=8 * 2**20, transcendentals=0),
        name="early",
    )(tokens, w_query, pair)

    keys = BLOCK + (GROUP - 1) * (rows // POOL) + spread.shape[0]
    s_late = [pltpu.VMEM((keys, stack), F32), pltpu.VMEM((1, stack), F32)]
    return pl.pallas_call(
        late,
        out_shape=shape((rows, w_out.shape[1]), BF16),
        in_specs=[VMEM] * 11,
        out_specs=VMEM,
        scratch_shapes=[
            pltpu.VMEM((blocks, KV_HEADS, keys, WIDE), BF16),
            pltpu.VMEM((blocks, KV_HEADS, VROWS, keys), BF16),
            pltpu.VMEM((blocks, HEADS * HEAD_DIM, BLOCK), BF16),
        ]
        + s_late
        + s_late,
        compiler_params=params(40),
        cost_estimate=pl.CostEstimate(flops=12 * 10**9, bytes_accessed=8 * 2**20, transcendentals=0),
        name="late",
    )(q, acc, top, before, after, *received, spread, w_out)


def solution(mesh):
    placed = (P("seq", None), P(), P(), P(), P())
    return jax.shard_map(body, mesh=mesh, in_specs=placed, out_specs=P("seq", None), check_vma=False)
```

```python
import functools
import math

import jax
import jax.numpy as jnp
from jax import lax
from jax.experimental import pallas as pl
from jax.experimental.pallas import tpu as pltpu
from jax.sharding import PartitionSpec as P

HEADS = 16
KV_HEADS = 4
HEAD_DIM = 64
BLOCK = 256
POOL = 16
GROUP = 16
SHARE = HEADS // KV_HEADS
WIDE = 128
VROWS = 80
BF16 = jnp.bfloat16
F32 = jnp.float32
NT = (((1,), (1,)), ((), ()))
TN = (((0,), (0,)), ((), ()))
MASKED = -1e30
HOPS = (2, 4, 8, 1)
VMEM = pl.BlockSpec(memory_space=pltpu.VMEM)
HBM = pl.BlockSpec(memory_space=pl.ANY)


def swap(rows, apart):
    count = lax.axis_size("seq")
    return lax.ppermute(rows, "seq", [(i, i ^ apart) for i in range(count)])


def place(slot):
    return sum(hop for bit, hop in enumerate(HOPS) if slot >> bit & 1)


def tied(rows, *others):
    return lax.optimization_barrier((rows, *others))[0]


def project_pair(tokens_hbm, wk_hbm, wv_hbm, tokens_ref, pair_ref, mid_ref, coarse_ref, inner_ref, outer_ref, wk_ref, wv_ref, sems):
    copies = [
        pltpu.make_async_copy(source, target, sems.at[at])
        for at, (source, target) in enumerate(((wk_hbm, wk_ref), (tokens_hbm, tokens_ref), (wv_hbm, wv_ref)))
    ]
    for copy in copies:
        copy.start()
    copies[0].wait()
    copies[1].wait()
    tokens = tokens_ref[...]
    rows = tokens.shape[0]
    width = wk_ref.shape[1]
    for part, weight in enumerate((wk_ref, wv_ref)):
        if part == 1:
            copies[2].wait()
        at = slice(part * width, (part + 1) * width)
        held = jnp.dot(tokens, weight[...], preferred_element_type=F32).astype(BF16)
        pair_ref[:, at] = held
        for factor, target in ((POOL, mid_ref), (BLOCK, coarse_ref)):
            kept = target.shape[0]
            first = lax.broadcasted_iota(jnp.int32, (kept, rows), 0) * factor
            inside = lax.broadcasted_iota(jnp.int32, (kept, rows), 1) - first
            share = jnp.where((inside >= 0) & (inside < factor), 1.0 / factor, 0.0)
            mean = jnp.dot(share.astype(BF16), held, preferred_element_type=F32)
            target[:, at] = mean.astype(BF16)
    even = lax.axis_index("seq") % 2 == 0
    inner_ref[...] = jnp.where(even, pair_ref[rows - BLOCK :], pair_ref[:BLOCK])
    outer_ref[...] = jnp.where(even, pair_ref[:BLOCK], pair_ref[rows - BLOCK :])


def put_keys(keys_ref, rows, at, count, biases):
    lane = lax.broadcasted_iota(jnp.int32, (count, HEAD_DIM), 1)
    extra = jnp.zeros((count, HEAD_DIM), F32)
    for place_, bias in enumerate(biases):
        extra = jnp.where(lane == place_, bias, extra)
    extra = extra.astype(BF16)
    for head in range(KV_HEADS):
        keys_ref[head, at : at + count, :HEAD_DIM] = rows[:, head * HEAD_DIM : (head + 1) * HEAD_DIM]
        keys_ref[head, at : at + count, HEAD_DIM:] = extra


def put_values(values_ref, rows):
    width = KV_HEADS * HEAD_DIM
    count = rows.shape[0]
    tall = KV_HEADS * VROWS
    row = lax.broadcasted_iota(jnp.int32, (tall, width), 0)
    column = lax.broadcasted_iota(jnp.int32, (tall, width), 1)
    head, inner = column // HEAD_DIM, column % HEAD_DIM
    pick = jnp.where(row == head * VROWS + inner, 1.0, 0.0).astype(BF16)
    turned = lax.dot_general(pick, rows, NT, preferred_element_type=F32)
    counting = lax.broadcasted_iota(jnp.int32, (tall, count), 0) % VROWS == HEAD_DIM
    values_ref[...] = jnp.where(counting, 1.0, turned).astype(BF16).reshape(KV_HEADS, VROWS, count)


def run_units(units, scores, finish, values, even, odd):
    def first(unit, buffers):
        held, top = buffers
        x, floor = scores(unit)
        held[...] = x
        highest = jnp.max(x, axis=0, keepdims=True)
        top[...] = highest if floor is None else jnp.maximum(highest, floor)

    def second(unit, buffers):
        held, top = buffers
        highest = top[...]
        weights = jnp.exp(held[...] - highest).astype(BF16)
        finish(unit, highest, jnp.dot(values(unit), weights, preferred_element_type=F32))

    first(0, even)

    def step(i, carry):
        first(2 * i + 1, odd)
        second(2 * i, even)
        first(2 * i + 2, even)
        second(2 * i + 1, odd)
        return carry

    lax.fori_loop(0, units // 2 - 1, step, 0)
    first(units - 1, odd)
    second(units - 2, even)
    second(units - 1, odd)


def own(groups, tokens_ref, wq_hbm, pair_ref, *rest):
    q_ref, acc_ref, top_ref, wq_ref, sems, keys_ref, values_ref, sa, ta, sb, tb = rest[-11:]
    rows = tokens_ref.shape[0]
    blocks = rows // BLOCK
    width = KV_HEADS * HEAD_DIM
    span = SHARE * HEAD_DIM
    copies = []
    for at, group in enumerate(groups):
        copy = pltpu.make_async_copy(wq_hbm.at[:, pl.ds(group * span, span)], wq_ref.at[at], sems.at[at])
        copy.start()
        copies.append(copy)
    put_keys(keys_ref, pair_ref[:, :width], 0, rows, ())
    put_values(values_ref, pair_ref[:, width:])
    lane = lax.broadcasted_iota(jnp.int32, (BLOCK, HEAD_DIM), 1)
    for at, group in enumerate(groups):
        copies[at].wait()
        part = jnp.dot(tokens_ref[...], wq_ref[at], preferred_element_type=F32)
        part = part.astype(BF16) * (1.0 / math.sqrt(HEAD_DIM))
        for block in range(blocks):
            extra = jnp.where(lane == block, 1.0, 0.0).astype(BF16)
            for head in range(SHARE):
                to = slice(head * BLOCK, (head + 1) * BLOCK)
                piece = part[block * BLOCK : (block + 1) * BLOCK, head * HEAD_DIM : (head + 1) * HEAD_DIM]
                q_ref[group * blocks + block, to, :HEAD_DIM] = piece
                q_ref[group * blocks + block, to, HEAD_DIM:] = extra
    start = groups[0] * blocks

    def scores(unit):
        unit = unit + start
        return lax.dot_general(keys_ref[unit // blocks], q_ref[unit], NT, preferred_element_type=F32), None

    def finish(unit, highest, total):
        acc_ref[unit + start] = total
        top_ref[unit + start] = highest

    run_units(len(groups) * blocks, scores, finish, lambda unit: values_ref[(unit + start) // blocks], (sa, ta), (sb, tb))


def halo(q_ref, acc_in, top_in, inner_ref, outer_ref, acc_ref, top_ref, keys_ref, values_ref, sa, ta, sb, tb):
    blocks = keys_ref.shape[0]
    width = KV_HEADS * HEAD_DIM
    me = lax.axis_index("seq")
    devices = lax.axis_size("seq")
    even = me % 2 == 0
    for block in range(blocks):
        exists = me > 0 if block == 0 else me < devices - 1
        rows = jnp.where(even == (block == 0), outer_ref[...], inner_ref[...])
        bias = jnp.where(exists, 0.0, MASKED)
        put_keys(keys_ref.at[block], rows[:, :width], 0, BLOCK, [bias] * blocks)
        put_values(values_ref.at[block], rows[:, width:])

    def scores(unit):
        x = lax.dot_general(keys_ref[unit % blocks, unit // blocks], q_ref[unit], NT, preferred_element_type=F32)
        return x, top_in[unit]

    def finish(unit, highest, total):
        acc_ref[unit] = total + acc_in[unit] * jnp.exp(top_in[unit] - highest)
        top_ref[unit] = highest

    run_units(KV_HEADS * blocks, scores, finish, lambda unit: values_ref[unit % blocks, unit // blocks], (sa, ta), (sb, tb))


def slot_owner(slot):
    owner = jnp.zeros_like(slot)
    for bit, hop in enumerate(HOPS):
        owner = owner + (slot // 2**bit % 2) * hop
    return owner


def far(q_ref, acc_ref, top_ref, x_ref, y_ref, z_ref, c_ref, far_ref, wout_hbm,
        out_hbm, wout_ref, out_ref, sems, keys_ref, values_ref, mixed_ref, sa, ta, sb, tb):
    fetch = pltpu.make_async_copy(wout_hbm, wout_ref, sems.at[0])
    fetch.start()
    blocks = mixed_ref.shape[0]
    width = KV_HEADS * HEAD_DIM
    me = lax.axis_index("seq")
    groups = lax.axis_size("seq") // GROUP
    runs = BLOCK // POOL
    per_device = runs * blocks
    far_rows = far_ref.shape[0]
    pieces = [(far_ref, far_rows), (x_ref, per_device), (y_ref, 2 * per_device), (z_ref, 4 * per_device), (c_ref, 8 * per_device)]
    spread = blocks * (groups - 1)
    row = lax.broadcasted_iota(jnp.int32, (far_rows, HEAD_DIM), 0)
    other = (row % spread) // blocks + 1
    far_block = (((me // GROUP) ^ other) * GROUP + ((me % GROUP) ^ slot_owner(row // spread))) * blocks + row % blocks
    row = lax.broadcasted_iota(jnp.int32, ((GROUP - 1) * per_device, HEAD_DIM), 0) + per_device
    mid_block = (me ^ slot_owner(row // per_device)) * blocks + row % per_device // runs
    indices = [me * blocks + block for block in range(blocks)]
    far_bias = [jnp.where(jnp.abs(far_block - index) > 1, 0.0, MASKED) for index in indices]
    mid_bias = [jnp.where(jnp.abs(mid_block - index) > 1, 0.0, MASKED) for index in indices]
    put_keys(keys_ref, far_ref[:, :width], 0, far_rows, far_bias)
    at = 0
    for piece, count in pieces[1:]:
        put_keys(keys_ref, piece[:count, :width], far_rows + at, count, [bias[at : at + count] for bias in mid_bias])
        at += count
    put_values(values_ref, jnp.concatenate([piece[:count, width:] for piece, count in pieces], axis=0))

    def scores(unit):
        return lax.dot_general(keys_ref[unit // blocks], q_ref[unit], NT, preferred_element_type=F32), top_ref[unit]

    def finish(unit, highest, total):
        total = total + acc_ref[unit] * jnp.exp(top_ref[unit] - highest)
        share = total[:HEAD_DIM] / total[HEAD_DIM : HEAD_DIM + 1]
        share = share.astype(BF16)
        for head in range(SHARE):
            to = pl.multiple_of((unit // blocks * SHARE + head) * HEAD_DIM, HEAD_DIM)
            mixed_ref[unit % blocks, pl.ds(to, HEAD_DIM), :] = share[:, head * BLOCK : (head + 1) * BLOCK]

    run_units(KV_HEADS * blocks, scores, finish, lambda unit: values_ref[unit // blocks], (sa, ta), (sb, tb))
    fetch.wait()
    stores = []
    for block in range(blocks):
        at = pl.ds(block * BLOCK, BLOCK)
        out_ref[at] = lax.dot_general(mixed_ref[block], wout_ref[...], TN, preferred_element_type=F32).astype(BF16)
        store = pltpu.make_async_copy(out_ref.at[at], out_hbm.at[at], sems.at[1 + block])
        store.start()
        stores.append(store)
    for store in stores:
        store.wait()


def body(tokens, w_query, w_key, w_value, w_out):
    devices = lax.axis_size("seq")
    rows, model = tokens.shape
    blocks = rows // BLOCK
    width = KV_HEADS * HEAD_DIM
    units = KV_HEADS * blocks
    stack = SHARE * BLOCK
    shape = jax.ShapeDtypeStruct
    dma = pltpu.SemaphoreType.DMA

    def call(kernel, out_shape, in_specs, out_specs, scratch, flops, name, aliases={}, mib=20):
        return pl.pallas_call(
            kernel,
            out_shape=out_shape,
            in_specs=in_specs,
            out_specs=out_specs,
            scratch_shapes=scratch,
            input_output_aliases=aliases,
            compiler_params=pltpu.CompilerParams(vmem_limit_bytes=mib * 2**20),
            cost_estimate=pl.CostEstimate(flops=flops, bytes_accessed=2**20, transcendentals=0),
            name=name,
        )

    def slots(keys):
        return [pltpu.VMEM((keys, stack), F32), pltpu.VMEM((1, stack), F32)] * 2

    half = shape((BLOCK, 2 * width), BF16)
    held_tokens, pair, mid, coarse, inner, outer = call(
        project_pair,
        [shape((rows, model), BF16), shape((rows, 2 * width), BF16), shape((rows // POOL, 2 * width), BF16), shape((blocks, 2 * width), BF16), half, half],
        [HBM] * 3,
        [VMEM] * 6,
        [pltpu.VMEM((model, width), BF16)] * 2 + [dma((3,))],
        2 * 10**9,
        "pair",
    )(tokens, w_key, w_value)

    spread = coarse
    level = GROUP
    while level < devices:
        spread = jnp.concatenate([spread, swap(spread, level)], axis=0)
        level *= 2
    spread = spread[blocks:]
    inner = swap(inner, 1)
    pairs = [(i, i + 1) for i in range(1, devices - 1, 2)]
    outer = lax.ppermute(outer, "seq", pairs + [(b, a) for a, b in pairs])
    held = mid
    payload = jnp.concatenate([held, spread], axis=0)
    first = swap(payload, HOPS[0])
    received = [first]

    state = [shape((units, stack, WIDE), BF16), shape((units, VROWS, stack), F32), shape((units, 1, stack), F32)]
    share = KV_HEADS // 2
    scratch = [
        pltpu.VMEM((share, model, SHARE * HEAD_DIM), BF16),
        dma((share,)),
        pltpu.VMEM((KV_HEADS, rows, WIDE), BF16),
        pltpu.VMEM((KV_HEADS, VROWS, rows), BF16),
    ] + slots(rows)
    attend = lambda part, extra: call(
        functools.partial(own, list(range(part * share, (part + 1) * share))),
        state,
        [VMEM, HBM, VMEM] + [VMEM] * extra,
        [VMEM] * 3,
        scratch,
        5 * 10**9,
        "own%d" % part,
        {3 + i: i for i in range(extra)},
    )
    q, acc, top = attend(0, 0)(tied(held_tokens, payload), w_query, pair)

    def grow(held, spread, both, hop, top):
        held = jnp.concatenate([held, both[: held.shape[0]]], axis=0)
        spread = jnp.concatenate([spread, both[held.shape[0] // 2 :]], axis=0)
        payload = tied(jnp.concatenate([held, spread], axis=0), top)
        both = swap(payload, hop)
        received.append(both)
        return held, spread, payload, both

    held, spread, payload, both = grow(held, spread, first, HOPS[1], top)
    q, acc, top = attend(1, 3)(tied(held_tokens, payload), w_query, pair, q, acc, top)
    held, spread, payload, both = grow(held, spread, both, HOPS[2], top)
    acc, top = call(
        halo,
        state[1:],
        [VMEM] * 5,
        [VMEM] * 2,
        [pltpu.VMEM((blocks, KV_HEADS, BLOCK, WIDE), BF16), pltpu.VMEM((blocks, KV_HEADS, VROWS, BLOCK), BF16)] + slots(BLOCK),
        4 * 10**9,
        "halo",
        {1: 0, 2: 1},
    )(tied(q, payload), acc, top, inner, outer)
    held, spread, payload, both = grow(held, spread, both, HOPS[3], top)
    spread = jnp.concatenate([spread, both[held.shape[0] :]], axis=0)
    keys = (GROUP - 1) * (rows // POOL) + spread.shape[0]
    return call(
        far,
        shape((rows, w_out.shape[1]), BF16),
        [VMEM] * 8 + [HBM],
        HBM,
        [
            pltpu.VMEM(w_out.shape, BF16),
            pltpu.VMEM((rows, w_out.shape[1]), BF16),
            dma((1 + blocks,)),
            pltpu.VMEM((KV_HEADS, keys, WIDE), BF16),
            pltpu.VMEM((KV_HEADS, VROWS, keys), BF16),
            pltpu.VMEM((blocks, HEADS * HEAD_DIM, BLOCK), BF16),
        ]
        + slots(keys),
        8 * 10**9,
        "far",
        mib=30,
    )(q, acc, top, *received, spread, w_out)


def solution(mesh):
    placed = (P("seq", None), P(), P(), P(), P())
    return jax.shard_map(body, mesh=mesh, in_specs=placed, out_specs=P("seq", None), check_vma=False)
```

```python
import math

import jax
import jax.numpy as jnp
from jax import lax
from jax.experimental import pallas as pl
from jax.experimental.pallas import tpu as pltpu
from jax.sharding import PartitionSpec as P

HEADS = 16
KV_HEADS = 4
HEAD_DIM = 64
BLOCK = 256
POOL = 16
GROUP = 16
SHARE = HEADS // KV_HEADS
WIDE = 128
VROWS = 80
BF16 = jnp.bfloat16
F32 = jnp.float32
NT = (((1,), (1,)), ((), ()))
TN = (((0,), (0,)), ((), ()))
MASKED = -1e30
VMEM = pl.BlockSpec(memory_space=pltpu.VMEM)
HBM = pl.BlockSpec(memory_space=pltpu.HBM)


def swap(rows, apart):
    count = lax.axis_size("seq")
    return lax.ppermute(rows, "seq", [(i, i ^ apart) for i in range(count)])


def tied(rows, *others):
    return lax.optimization_barrier((rows, *others))[0]


def project_pair(tokens_hbm, wk_hbm, wv_hbm, pair_ref, mid_ref, coarse_ref, inner_ref, outer_ref, tokens_ref, wk_ref, wv_ref, sems):
    copies = [
        pltpu.make_async_copy(source, target, sems.at[at])
        for at, (source, target) in enumerate(((wk_hbm, wk_ref), (tokens_hbm, tokens_ref), (wv_hbm, wv_ref)))
    ]
    for copy in copies:
        copy.start()
    copies[0].wait()
    copies[1].wait()
    tokens = tokens_ref[...]
    rows = tokens.shape[0]
    width = wk_ref.shape[1]
    for part, weight in enumerate((wk_ref, wv_ref)):
        if part == 1:
            copies[2].wait()
        at = slice(part * width, (part + 1) * width)
        held = jnp.dot(tokens, weight[...], preferred_element_type=F32).astype(BF16)
        pair_ref[:, at] = held
        for factor, target in ((POOL, mid_ref), (BLOCK, coarse_ref)):
            kept = target.shape[0]
            first = lax.broadcasted_iota(jnp.int32, (kept, rows), 0) * factor
            inside = lax.broadcasted_iota(jnp.int32, (kept, rows), 1) - first
            share = jnp.where((inside >= 0) & (inside < factor), 1.0 / factor, 0.0)
            mean = jnp.dot(share.astype(BF16), held, preferred_element_type=F32)
            target[:, at] = mean.astype(BF16)
    even = lax.axis_index("seq") % 2 == 0
    inner_ref[...] = jnp.where(even, pair_ref[rows - BLOCK :], pair_ref[:BLOCK])
    outer_ref[...] = jnp.where(even, pair_ref[:BLOCK], pair_ref[rows - BLOCK :])


def put_keys(keys_ref, rows, at, biases):
    count = rows.shape[0]
    lane = lax.broadcasted_iota(jnp.int32, (count, HEAD_DIM), 1)
    extra = jnp.zeros((count, HEAD_DIM), F32)
    for order, bias in enumerate(biases):
        extra = jnp.where(lane == order, bias, extra)
    extra = extra.astype(BF16)
    for head in range(KV_HEADS):
        keys_ref[head, pl.ds(at, count), :HEAD_DIM] = rows[:, head * HEAD_DIM : (head + 1) * HEAD_DIM]
        keys_ref[head, pl.ds(at, count), HEAD_DIM:] = extra


def put_values(values_ref, rows):
    width = KV_HEADS * HEAD_DIM
    count = rows.shape[0]
    tall = KV_HEADS * VROWS
    row = lax.broadcasted_iota(jnp.int32, (tall, width), 0)
    column = lax.broadcasted_iota(jnp.int32, (tall, width), 1)
    head, inner = column // HEAD_DIM, column % HEAD_DIM
    pick = jnp.where(row == head * VROWS + inner, 1.0, 0.0).astype(BF16)
    turned = lax.dot_general(pick, rows, NT, preferred_element_type=F32)
    counting = lax.broadcasted_iota(jnp.int32, (tall, count), 0) % VROWS == HEAD_DIM
    values_ref[...] = jnp.where(counting, 1.0, turned).astype(BF16).reshape(KV_HEADS, VROWS, count)


def run_units(scores, finish, values, buffers):
    def first(group, block):
        held, top = buffers[block]
        x, floor = scores(group, block)
        held[...] = x
        highest = jnp.max(x, axis=0, keepdims=True)
        top[...] = highest if floor is None else jnp.maximum(highest, floor)

    def second(group, block):
        held, top = buffers[block]
        highest = top[...]
        weights = jnp.exp(held[...] - highest).astype(BF16)
        finish(group, block, highest, jnp.dot(values(group, block), weights, preferred_element_type=F32))

    first(0, 0)

    def step(group, carry):
        first(group, 1)
        second(group, 0)
        first(group + 1, 0)
        second(group, 1)
        return carry

    lax.fori_loop(0, KV_HEADS - 1, step, 0)
    last = KV_HEADS - 1
    first(last, 1)
    second(last, 0)
    second(last, 1)


def near(tokens_hbm, wq_hbm, pair_ref, inner_ref, outer_ref, q_hbm, acc_hbm, top_hbm,
         tokens_ref, wq_ref, q_ref, acc_ref, top_ref, sems, keys_ref, values_ref, sa, ta, sb, tb):
    rows = tokens_ref.shape[0]
    blocks = rows // BLOCK
    width = KV_HEADS * HEAD_DIM
    span = SHARE * HEAD_DIM
    me = lax.axis_index("seq")
    devices = lax.axis_size("seq")
    even = me % 2 == 0
    fetches = [pltpu.make_async_copy(tokens_hbm, tokens_ref, sems.at[KV_HEADS])]
    for group in range(KV_HEADS):
        fetches.append(pltpu.make_async_copy(wq_hbm.at[:, pl.ds(group * span, span)], wq_ref.at[group], sems.at[group]))
    for fetch in fetches:
        fetch.start()
    prev = jnp.where(even, outer_ref[...], inner_ref[...])
    follow = jnp.where(even, inner_ref[...], outer_ref[...])
    put_keys(keys_ref, prev[:, :width], 0, [jnp.where(me > 0, 0.0, MASKED)] * blocks)
    put_keys(keys_ref, pair_ref[:, :width], BLOCK, ())
    put_keys(keys_ref, follow[:, :width], BLOCK + rows, [jnp.where(me < devices - 1, 0.0, MASKED)] * blocks)
    put_values(values_ref, jnp.concatenate([prev[:, width:], pair_ref[:, width:], follow[:, width:]], axis=0))
    fetches[0].wait()
    lane = lax.broadcasted_iota(jnp.int32, (BLOCK, HEAD_DIM), 1)
    for group in range(KV_HEADS):
        fetches[1 + group].wait()
        part = jnp.dot(tokens_ref[...], wq_ref[group], preferred_element_type=F32)
        part = part.astype(BF16) * (1.0 / math.sqrt(HEAD_DIM))
        for block in range(blocks):
            extra = jnp.where(lane == block, 1.0, 0.0).astype(BF16)
            for head in range(SHARE):
                to = slice(head * BLOCK, (head + 1) * BLOCK)
                piece = part[block * BLOCK : (block + 1) * BLOCK, head * HEAD_DIM : (head + 1) * HEAD_DIM]
                q_ref[group, block, to, :HEAD_DIM] = piece
                q_ref[group, block, to, HEAD_DIM:] = extra
    keep = pltpu.make_async_copy(q_ref, q_hbm, sems.at[KV_HEADS + 1])
    keep.start()

    def scores(group, block):
        at = slice(block * BLOCK, block * BLOCK + BLOCK + rows)
        return lax.dot_general(keys_ref[group, at], q_ref[group, block], NT, preferred_element_type=F32), None

    def kept(group):
        return pltpu.make_async_copy(acc_ref.at[group], acc_hbm.at[group], sems.at[KV_HEADS + 2])

    def finish(group, block, highest, total):
        acc_ref[group, block] = total
        top_ref[group, block] = highest
        if block == blocks - 1:
            kept(group).start()

    def values(group, block):
        return values_ref[group, :, block * BLOCK : block * BLOCK + BLOCK + rows]

    run_units(scores, finish, values, ((sa, ta), (sb, tb)))
    keep_top = pltpu.make_async_copy(top_ref, top_hbm, sems.at[0])
    keep_top.start()
    keep.wait()
    pltpu.make_async_copy(acc_ref, acc_hbm, sems.at[KV_HEADS + 2]).wait()
    keep_top.wait()


def far(q_hbm, acc_hbm, top_hbm, mids_ref, coarse_ref, wout_hbm, out_hbm,
        q_ref, acc_ref, top_ref, wout_ref, out_ref, sems, rows_ref, keys_ref, values_ref, mixed_ref, sa, ta, sb, tb):
    fetches = [
        pltpu.make_async_copy(source, target, sems.at[at])
        for at, (source, target) in enumerate(
            ((q_hbm, q_ref), (top_hbm, top_ref), (acc_hbm, acc_ref), (wout_hbm, wout_ref))
        )
    ]
    for fetch in fetches:
        fetch.start()
    blocks = mixed_ref.shape[0]
    width = KV_HEADS * HEAD_DIM
    me = lax.axis_index("seq")
    groups = lax.axis_size("seq") // GROUP
    mine = me % GROUP
    runs = BLOCK // POOL
    per_device = runs * blocks
    mid_rows = GROUP * per_device
    spread = blocks * (groups - 1)
    swapped = pl.multiple_of(mine * per_device, per_device)
    for member in range(GROUP):
        rows_ref[member * per_device : (member + 1) * per_device] = mids_ref[member, :per_device]
    rows_ref[pl.ds(swapped, per_device)] = coarse_ref[:per_device]
    if coarse_ref.shape[0] > per_device:
        rows_ref[mid_rows:] = coarse_ref[per_device:]
    indices = [me * blocks + block for block in range(blocks)]
    row = lax.broadcasted_iota(jnp.int32, (mid_rows, HEAD_DIM), 0)
    mid_block = (me - mine + row // per_device) * blocks + row % per_device // runs
    put_keys(keys_ref, rows_ref[:mid_rows, :width], 0, [jnp.where(jnp.abs(mid_block - index) > 1, 0.0, MASKED) for index in indices])
    for start in range(0, coarse_ref.shape[0], per_device):
        row = lax.broadcasted_iota(jnp.int32, (per_device, HEAD_DIM), 0) + start
        other = (row % spread) // blocks + 1
        far_block = (((me // GROUP) ^ other) * GROUP + row // spread) * blocks + row % blocks
        bias = [jnp.where(jnp.abs(far_block - index) > 1, 0.0, MASKED) for index in indices]
        at = swapped if start == 0 else mid_rows + start - per_device
        put_keys(keys_ref, coarse_ref[start : start + per_device, :width], at, bias)
    put_values(values_ref, rows_ref[:, width:])
    fetches[0].wait()
    fetches[1].wait()
    fetches[2].wait()

    def scores(group, block):
        return lax.dot_general(keys_ref[group], q_ref[group, block], NT, preferred_element_type=F32), top_ref[group, block]

    def finish(group, block, highest, total):
        total = total + acc_ref[group, block] * jnp.exp(top_ref[group, block] - highest)
        share = total[:HEAD_DIM] / total[HEAD_DIM : HEAD_DIM + 1]
        share = share.astype(BF16)
        for head in range(SHARE):
            to = pl.multiple_of((group * SHARE + head) * HEAD_DIM, HEAD_DIM)
            mixed_ref[block, pl.ds(to, HEAD_DIM), :] = share[:, head * BLOCK : (head + 1) * BLOCK]

    run_units(scores, finish, lambda group, block: values_ref[group], ((sa, ta), (sb, tb)))
    fetches[3].wait()
    stores = []
    for block in range(blocks):
        at = pl.ds(block * BLOCK, BLOCK)
        out_ref[at] = lax.dot_general(mixed_ref[block], wout_ref[...], TN, preferred_element_type=F32).astype(BF16)
        store = pltpu.make_async_copy(out_ref.at[at], out_hbm.at[at], sems.at[4 + block])
        store.start()
        stores.append(store)
    for store in stores:
        store.wait()


def body(tokens, w_query, w_key, w_value, w_out):
    devices = lax.axis_size("seq")
    rows, model = tokens.shape
    blocks = rows // BLOCK
    width = KV_HEADS * HEAD_DIM
    stack = SHARE * BLOCK
    per_device = rows // POOL
    shape = jax.ShapeDtypeStruct
    dma = pltpu.SemaphoreType.DMA

    def call(kernel, out_shape, in_specs, out_specs, scratch, flops, name, kib=53000):
        return pl.pallas_call(
            kernel,
            out_shape=out_shape,
            in_specs=in_specs,
            out_specs=out_specs,
            scratch_shapes=scratch,
            compiler_params=pltpu.CompilerParams(vmem_limit_bytes=kib * 2**10),
            cost_estimate=pl.CostEstimate(flops=flops, bytes_accessed=2**20, transcendentals=0),
            name=name,
        )

    def slots(keys):
        return [pltpu.VMEM((keys, stack), F32), pltpu.VMEM((1, stack), F32)] * 2

    half = shape((BLOCK, 2 * width), BF16)
    pair, mid, coarse, inner, outer = call(
        project_pair,
        [shape((rows, 2 * width), BF16), shape((per_device, 2 * width), BF16), shape((blocks, 2 * width), BF16), half, half],
        [HBM] * 3,
        [VMEM] * 5,
        [pltpu.VMEM((rows, model), BF16)] + [pltpu.VMEM((model, width), BF16)] * 2 + [dma((3,))],
        2 * 10**9,
        "pair",
        54000,
    )(tokens, w_key, w_value)

    spread = coarse
    level = GROUP
    while level < devices:
        spread = jnp.concatenate([spread, swap(spread, level)], axis=0)
        level *= 2
    spread = spread[blocks:]
    inner = swap(inner, 1)
    links = [(i, i + 1) for i in range(1, devices - 1, 2)]
    outer = lax.ppermute(outer, "seq", links + [(b, a) for a, b in links])
    payload = jnp.concatenate([mid, spread], axis=0)
    payload = jnp.broadcast_to(payload[None], (GROUP, *payload.shape))
    members = [list(range(at, at + GROUP)) for at in range(0, devices, GROUP)]
    arrived = lax.all_to_all(payload, "seq", 0, 0, axis_index_groups=members)

    state = [shape((KV_HEADS, blocks, stack, WIDE), BF16), shape((KV_HEADS, blocks, VROWS, stack), F32), shape((KV_HEADS, blocks, 1, stack), F32)]
    held = [pltpu.VMEM(part.shape, part.dtype) for part in state]
    q, acc, top = call(
        near,
        state,
        [HBM, HBM, VMEM, VMEM, VMEM],
        [HBM] * 3,
        [pltpu.VMEM((rows, model), BF16), pltpu.VMEM((KV_HEADS, model, SHARE * HEAD_DIM), BF16)]
        + held
        + [dma((KV_HEADS + 3,)), pltpu.VMEM((KV_HEADS, rows + 2 * BLOCK, WIDE), BF16), pltpu.VMEM((KV_HEADS, VROWS, rows + 2 * BLOCK), BF16)]
        + slots(rows + BLOCK),
        10**10,
        "near",
    )(tokens, w_query, tied(pair, payload), inner, outer)

    coarse_far = arrived[:, per_device:].reshape(-1, 2 * width)
    keys = (GROUP - 1) * per_device + coarse_far.shape[0]
    return call(
        far,
        shape((rows, w_out.shape[1]), BF16),
        [HBM] * 3 + [VMEM, VMEM, HBM],
        HBM,
        held
        + [
            pltpu.VMEM(w_out.shape, BF16),
            pltpu.VMEM((rows, w_out.shape[1]), BF16),
            dma((4 + blocks,)),
            pltpu.VMEM((keys, 2 * width), BF16),
            pltpu.VMEM((KV_HEADS, keys, WIDE), BF16),
            pltpu.VMEM((KV_HEADS, VROWS, keys), BF16),
            pltpu.VMEM((blocks, HEADS * HEAD_DIM, BLOCK), BF16),
        ]
        + slots(keys),
        8 * 10**9,
        "far",
    )(q, acc, top, arrived, coarse_far, w_out)


def solution(mesh):
    placed = (P("seq", None), P(), P(), P(), P())
    return jax.shard_map(body, mesh=mesh, in_specs=placed, out_specs=P("seq", None), check_vma=False)
```

```python
import math

import jax
import jax.numpy as jnp
from jax import lax
from jax.experimental import pallas as pl
from jax.experimental.pallas import tpu as pltpu
from jax.sharding import PartitionSpec as P

HEADS = 16
KV_HEADS = 4
HEAD_DIM = 64
BLOCK = 256
POOL = 16
GROUP = 16
SHARE = HEADS // KV_HEADS
WIDE = 128
VROWS = 80
BF16 = jnp.bfloat16
F32 = jnp.float32
NT = (((1,), (1,)), ((), ()))
TN = (((0,), (0,)), ((), ()))
MASKED = -1e30
VMEM = pl.BlockSpec(memory_space=pltpu.VMEM)
HBM = pl.BlockSpec(memory_space=pltpu.HBM)


def swap(rows, apart):
    count = lax.axis_size("seq")
    return lax.ppermute(rows, "seq", [(i, i ^ apart) for i in range(count)])


def tied(rows, *others):
    return lax.optimization_barrier((rows, *others))[0]


def project_pair(tokens_hbm, wk_hbm, wv_hbm, pair_ref, mid_ref, coarse_ref, inner_ref, outer_ref, tokens_ref, weight_ref, sems):
    rows = tokens_ref.shape[0]
    width = wk_hbm.shape[1]
    blocks = rows // BLOCK
    fetches = [pltpu.make_async_copy(wk_hbm, weight_ref.at[:, pl.ds(0, width)], sems.at[0])]
    fetches.append(pltpu.make_async_copy(wv_hbm, weight_ref.at[:, pl.ds(width, width)], sems.at[1]))
    for block in range(blocks):
        at = pl.ds(block * BLOCK, BLOCK)
        fetches.append(pltpu.make_async_copy(tokens_hbm.at[at], tokens_ref.at[at], sems.at[2 + block]))
    for fetch in fetches:
        fetch.start()
    even = lax.axis_index("seq") % 2 == 0
    runs = BLOCK // POOL
    tall = 3 * runs // 2
    row = lax.broadcasted_iota(jnp.int32, (tall, BLOCK), 0)
    column = lax.broadcasted_iota(jnp.int32, (tall, BLOCK), 1)
    share = jnp.where(row < runs, jnp.where(column // POOL == row, 1.0 / POOL, 0.0), jnp.where(row == runs, 1.0 / BLOCK, 0.0))
    share = share.astype(BF16)
    fetches[0].wait()
    fetches[1].wait()
    kept = []
    for block in range(blocks):
        at = slice(block * BLOCK, (block + 1) * BLOCK)
        fetches[2 + block].wait()
        held = jnp.dot(tokens_ref[at], weight_ref[...], preferred_element_type=F32).astype(BF16)
        pair_ref[at] = held
        kept.append(held)
        mean = jnp.dot(share, held, preferred_element_type=F32)
        mid_ref[block * runs : (block + 1) * runs] = mean[:runs].astype(BF16)
        coarse_ref[block : block + 1] = mean[runs : runs + 1].astype(BF16)
    inner_ref[...] = jnp.where(even, kept[-1], kept[0])
    outer_ref[...] = jnp.where(even, kept[0], kept[-1])


def query(tokens_hbm, wq_hbm, order_ref, q_hbm, tokens_ref, wq_ref, q_ref, sems):
    rows = tokens_ref.shape[0]
    blocks = rows // BLOCK
    span = SHARE * HEAD_DIM
    fetches = [pltpu.make_async_copy(tokens_hbm, tokens_ref, sems.at[KV_HEADS])]
    for group in range(KV_HEADS):
        fetches.append(pltpu.make_async_copy(wq_hbm.at[:, pl.ds(group * span, span)], wq_ref.at[group], sems.at[group]))
    for fetch in fetches:
        fetch.start()
    lane = lax.broadcasted_iota(jnp.int32, (BLOCK, HEAD_DIM), 1)
    fetches[0].wait()
    keeps = []
    for group in range(KV_HEADS):
        fetches[1 + group].wait()
        part = jnp.dot(tokens_ref[...], wq_ref[group], preferred_element_type=F32)
        part = part.astype(BF16) * (1.0 / math.sqrt(HEAD_DIM))
        for block in range(blocks):
            extra = jnp.where(lane == block, 1.0, 0.0).astype(BF16)
            for head in range(SHARE):
                to = slice(head * BLOCK, (head + 1) * BLOCK)
                piece = part[block * BLOCK : (block + 1) * BLOCK, head * HEAD_DIM : (head + 1) * HEAD_DIM]
                q_ref[group, block, to, :HEAD_DIM] = piece
                q_ref[group, block, to, HEAD_DIM:] = extra
        keeps.append(pltpu.make_async_copy(q_ref.at[group], q_hbm.at[group], sems.at[KV_HEADS + 1 + group]))
        keeps[-1].start()
    for keep in keeps:
        keep.wait()


def put_keys(keys_ref, rows, at, biases):
    count = rows.shape[0]
    lane = lax.broadcasted_iota(jnp.int32, (count, HEAD_DIM), 1)
    extra = jnp.zeros((count, HEAD_DIM), F32)
    for order, bias in enumerate(biases):
        extra = jnp.where(lane == order, bias, extra)
    extra = extra.astype(BF16)
    for head in range(KV_HEADS):
        keys_ref[head, pl.ds(at, count), :HEAD_DIM] = rows[:, head * HEAD_DIM : (head + 1) * HEAD_DIM]
        keys_ref[head, pl.ds(at, count), HEAD_DIM:] = extra


def put_values(values_ref, rows):
    width = KV_HEADS * HEAD_DIM
    count = rows.shape[0]
    tall = KV_HEADS * VROWS
    row = lax.broadcasted_iota(jnp.int32, (tall, width), 0)
    column = lax.broadcasted_iota(jnp.int32, (tall, width), 1)
    head, inner = column // HEAD_DIM, column % HEAD_DIM
    pick = jnp.where(row == head * VROWS + inner, 1.0, 0.0).astype(BF16)
    turned = lax.dot_general(pick, rows, NT, preferred_element_type=F32)
    counting = lax.broadcasted_iota(jnp.int32, (tall, count), 0) % VROWS == HEAD_DIM
    values_ref[...] = jnp.where(counting, 1.0, turned).astype(BF16).reshape(KV_HEADS, VROWS, count)


def run_units(scores, finish, values, buffers):
    def first(group, block):
        held, top = buffers[block]
        x, floor = scores(group, block)
        held[...] = x
        highest = jnp.max(x, axis=0, keepdims=True)
        top[...] = highest if floor is None else jnp.maximum(highest, floor)

    def second(group, block):
        held, top = buffers[block]
        highest = top[...]
        weights = jnp.exp(held[...] - highest).astype(BF16)
        finish(group, block, highest, jnp.dot(values(group, block), weights, preferred_element_type=F32))

    first(0, 0)

    def step(group, carry):
        first(group, 1)
        second(group, 0)
        first(group + 1, 0)
        second(group, 1)
        return carry

    lax.fori_loop(0, KV_HEADS - 1, step, 0)
    last = KV_HEADS - 1
    first(last, 1)
    second(last, 0)
    second(last, 1)


def near(q_hbm, pair_ref, inner_ref, outer_ref, acc_hbm, top_hbm,
         q_ref, acc_ref, top_ref, sems, keys_ref, values_ref, sa, ta, sb, tb):
    fetch = pltpu.make_async_copy(q_hbm, q_ref, sems.at[0])
    fetch.start()
    rows = pair_ref.shape[0]
    blocks = rows // BLOCK
    width = KV_HEADS * HEAD_DIM
    me = lax.axis_index("seq")
    devices = lax.axis_size("seq")
    even = me % 2 == 0
    prev = jnp.where(even, outer_ref[...], inner_ref[...])
    follow = jnp.where(even, inner_ref[...], outer_ref[...])
    put_keys(keys_ref, prev[:, :width], 0, [jnp.where(me > 0, 0.0, MASKED)] * blocks)
    put_keys(keys_ref, pair_ref[:, :width], BLOCK, ())
    put_keys(keys_ref, follow[:, :width], BLOCK + rows, [jnp.where(me < devices - 1, 0.0, MASKED)] * blocks)
    put_values(values_ref, jnp.concatenate([prev[:, width:], pair_ref[:, width:], follow[:, width:]], axis=0))
    fetch.wait()

    def scores(group, block):
        at = slice(block * BLOCK, block * BLOCK + BLOCK + rows)
        return lax.dot_general(keys_ref[group, at], q_ref[group, block], NT, preferred_element_type=F32), None

    def kept(group):
        return pltpu.make_async_copy(acc_ref.at[group], acc_hbm.at[group], sems.at[1])

    def finish(group, block, highest, total):
        acc_ref[group, block] = total
        top_ref[group, block] = highest
        if block == blocks - 1:
            kept(group).start()

    def values(group, block):
        return values_ref[group, :, block * BLOCK : block * BLOCK + BLOCK + rows]

    run_units(scores, finish, values, ((sa, ta), (sb, tb)))
    keep_top = pltpu.make_async_copy(top_ref, top_hbm, sems.at[0])
    keep_top.start()
    pltpu.make_async_copy(acc_ref, acc_hbm, sems.at[1]).wait()
    keep_top.wait()


def far(q_hbm, acc_hbm, top_hbm, mids_ref, coarse_ref, wout_hbm, out_hbm,
        q_ref, acc_ref, top_ref, wout_ref, out_ref, sems, rows_ref, keys_ref, values_ref, mixed_ref, sa, ta, sb, tb):
    fetches = [
        pltpu.make_async_copy(source, target, sems.at[at])
        for at, (source, target) in enumerate(
            ((q_hbm, q_ref), (top_hbm, top_ref), (acc_hbm, acc_ref), (wout_hbm, wout_ref))
        )
    ]
    for fetch in fetches:
        fetch.start()
    blocks = mixed_ref.shape[0]
    width = KV_HEADS * HEAD_DIM
    me = lax.axis_index("seq")
    groups = lax.axis_size("seq") // GROUP
    mine = me % GROUP
    runs = BLOCK // POOL
    per_device = runs * blocks
    mid_rows = GROUP * per_device
    spread = blocks * (groups - 1)
    swapped = pl.multiple_of(mine * per_device, per_device)
    for member in range(GROUP):
        rows_ref[member * per_device : (member + 1) * per_device] = mids_ref[member, :per_device]
    rows_ref[pl.ds(swapped, per_device)] = coarse_ref[:per_device]
    if coarse_ref.shape[0] > per_device:
        rows_ref[mid_rows:] = coarse_ref[per_device:]
    indices = [me * blocks + block for block in range(blocks)]
    row = lax.broadcasted_iota(jnp.int32, (mid_rows, HEAD_DIM), 0)
    mid_block = (me - mine + row // per_device) * blocks + row % per_device // runs
    put_keys(keys_ref, rows_ref[:mid_rows, :width], 0, [jnp.where(jnp.abs(mid_block - index) > 1, 0.0, MASKED) for index in indices])
    for start in range(0, coarse_ref.shape[0], per_device):
        row = lax.broadcasted_iota(jnp.int32, (per_device, HEAD_DIM), 0) + start
        other = (row % spread) // blocks + 1
        far_block = (((me // GROUP) ^ other) * GROUP + row // spread) * blocks + row % blocks
        bias = [jnp.where(jnp.abs(far_block - index) > 1, 0.0, MASKED) for index in indices]
        at = swapped if start == 0 else mid_rows + start - per_device
        put_keys(keys_ref, coarse_ref[start : start + per_device, :width], at, bias)
    put_values(values_ref, rows_ref[:, width:])
    for fetch in fetches[:3]:
        fetch.wait()

    def scores(group, block):
        return lax.dot_general(keys_ref[group], q_ref[group, block], NT, preferred_element_type=F32), top_ref[group, block]

    def finish(group, block, highest, total):
        total = total + acc_ref[group, block] * jnp.exp(top_ref[group, block] - highest)
        share = total[:HEAD_DIM] / total[HEAD_DIM : HEAD_DIM + 1]
        share = share.astype(BF16)
        for head in range(SHARE):
            to = pl.multiple_of((group * SHARE + head) * HEAD_DIM, HEAD_DIM)
            mixed_ref[block, pl.ds(to, HEAD_DIM), :] = share[:, head * BLOCK : (head + 1) * BLOCK]

    run_units(scores, finish, lambda group, block: values_ref[group], ((sa, ta), (sb, tb)))
    fetches[3].wait()
    stores = []
    for block in range(blocks):
        at = pl.ds(block * BLOCK, BLOCK)
        out_ref[at] = lax.dot_general(mixed_ref[block], wout_ref[...], TN, preferred_element_type=F32).astype(BF16)
        store = pltpu.make_async_copy(out_ref.at[at], out_hbm.at[at], sems.at[4 + block])
        store.start()
        stores.append(store)
    for store in stores:
        store.wait()


def body(tokens, w_query, w_key, w_value, w_out):
    devices = lax.axis_size("seq")
    rows, model = tokens.shape
    blocks = rows // BLOCK
    width = KV_HEADS * HEAD_DIM
    stack = SHARE * BLOCK
    per_device = rows // POOL
    shape = jax.ShapeDtypeStruct
    dma = pltpu.SemaphoreType.DMA

    def call(kernel, out_shape, in_specs, out_specs, scratch, flops, name, kib=53000):
        return pl.pallas_call(
            kernel,
            out_shape=out_shape,
            in_specs=in_specs,
            out_specs=out_specs,
            scratch_shapes=scratch,
            compiler_params=pltpu.CompilerParams(vmem_limit_bytes=kib * 2**10),
            cost_estimate=pl.CostEstimate(flops=flops, bytes_accessed=2**20, transcendentals=0),
            name=name,
        )

    def slots(keys):
        return [pltpu.VMEM((keys, stack), F32), pltpu.VMEM((1, stack), F32)] * 2

    half = shape((BLOCK, 2 * width), BF16)
    pair, mid, coarse, inner, outer = call(
        project_pair,
        [shape((rows, 2 * width), BF16), shape((per_device, 2 * width), BF16), shape((blocks, 2 * width), BF16), half, half],
        [HBM] * 3,
        [VMEM] * 5,
        [pltpu.VMEM((rows, model), BF16), pltpu.VMEM((model, 2 * width), BF16), dma((2 + blocks,))],
        2 * 10**9,
        "pair",
        54000,
    )(tokens, w_key, w_value)

    state = [shape((KV_HEADS, blocks, stack, WIDE), BF16), shape((KV_HEADS, blocks, VROWS, stack), F32), shape((KV_HEADS, blocks, 1, stack), F32)]
    held = [pltpu.VMEM(part.shape, part.dtype) for part in state]
    spread = coarse
    level = GROUP
    while level < devices:
        spread = jnp.concatenate([spread, swap(spread, level)], axis=0)
        level *= 2
    spread = spread[blocks:]
    inner = swap(inner, 1)
    q = call(
        query,
        state[0],
        [HBM, HBM, VMEM],
        HBM,
        [pltpu.VMEM((rows, model), BF16), pltpu.VMEM((KV_HEADS, model, SHARE * HEAD_DIM), BF16), held[0], dma((2 * KV_HEADS + 1,))],
        2 * 10**9,
        "query",
        55000,
    )(tokens, w_query, coarse)
    spread = tied(spread, q)
    links = [(i, i + 1) for i in range(1, devices - 1, 2)]
    outer = lax.ppermute(tied(outer, spread), "seq", links + [(b, a) for a, b in links])
    payload = jnp.concatenate([mid, spread], axis=0)
    payload = jnp.broadcast_to(payload[None], (GROUP, *payload.shape))
    members = [list(range(at, at + GROUP)) for at in range(0, devices, GROUP)]
    arrived = lax.all_to_all(payload, "seq", 0, 0, axis_index_groups=members)

    acc, top = call(
        near,
        state[1:],
        [HBM, VMEM, VMEM, VMEM],
        [HBM] * 2,
        held
        + [dma((2,)), pltpu.VMEM((KV_HEADS, rows + 2 * BLOCK, WIDE), BF16), pltpu.VMEM((KV_HEADS, VROWS, rows + 2 * BLOCK), BF16)]
        + slots(rows + BLOCK),
        10**10,
        "near",
    )(q, tied(pair, payload), inner, outer)

    coarse_far = arrived[:, per_device:].reshape(-1, 2 * width)
    keys = (GROUP - 1) * per_device + coarse_far.shape[0]
    return call(
        far,
        shape((rows, w_out.shape[1]), BF16),
        [HBM] * 3 + [VMEM, VMEM, HBM],
        HBM,
        held
        + [
            pltpu.VMEM(w_out.shape, BF16),
            pltpu.VMEM((rows, w_out.shape[1]), BF16),
            dma((4 + blocks,)),
            pltpu.VMEM((keys, 2 * width), BF16),
            pltpu.VMEM((KV_HEADS, keys, WIDE), BF16),
            pltpu.VMEM((KV_HEADS, VROWS, keys), BF16),
            pltpu.VMEM((blocks, HEADS * HEAD_DIM, BLOCK), BF16),
        ]
        + slots(keys),
        8 * 10**9,
        "far",
    )(q, acc, top, arrived, coarse_far, w_out)


def solution(mesh):
    placed = (P("seq", None), P(), P(), P(), P())
    return jax.shard_map(body, mesh=mesh, in_specs=placed, out_specs=P("seq", None), check_vma=False)
```

```python
import math

import jax
import jax.numpy as jnp
from jax import lax
from jax.experimental import pallas as pl
from jax.experimental.pallas import tpu as pltpu
from jax.sharding import PartitionSpec as P

HEADS = 16
KV_HEADS = 4
HEAD_DIM = 64
BLOCK = 256
POOL = 16
GROUP = 16
SHARE = HEADS // KV_HEADS
WIDE = 128
VROWS = 80
BF16 = jnp.bfloat16
F32 = jnp.float32
NT = (((1,), (1,)), ((), ()))
TN = (((0,), (0,)), ((), ()))
MASKED = -1e30
VMEM = pl.BlockSpec(memory_space=pltpu.VMEM)
HBM = pl.BlockSpec(memory_space=pltpu.HBM)


def swap(rows, apart):
    count = lax.axis_size("seq")
    return lax.ppermute(rows, "seq", [(i, i ^ apart) for i in range(count)])


def tied(rows, *others):
    return lax.optimization_barrier((rows, *others))[0]


def project_pair(tokens_hbm, wk_hbm, wv_hbm, pair_ref, mid_ref, coarse_ref, inner_ref, outer_ref, tokens_ref, weight_ref, sems):
    rows = tokens_ref.shape[0]
    width = wk_hbm.shape[1]
    blocks = rows // BLOCK
    fetches = [pltpu.make_async_copy(wk_hbm, weight_ref.at[:, pl.ds(0, width)], sems.at[0])]
    fetches.append(pltpu.make_async_copy(wv_hbm, weight_ref.at[:, pl.ds(width, width)], sems.at[1]))
    for block in range(blocks):
        at = pl.ds(block * BLOCK, BLOCK)
        fetches.append(pltpu.make_async_copy(tokens_hbm.at[at], tokens_ref.at[at], sems.at[2 + block]))
    for fetch in fetches:
        fetch.start()
    even = lax.axis_index("seq") % 2 == 0
    runs = BLOCK // POOL
    tall = 3 * runs // 2
    row = lax.broadcasted_iota(jnp.int32, (tall, BLOCK), 0)
    column = lax.broadcasted_iota(jnp.int32, (tall, BLOCK), 1)
    share = jnp.where(row < runs, jnp.where(column // POOL == row, 1.0 / POOL, 0.0), jnp.where(row == runs, 1.0 / BLOCK, 0.0))
    share = share.astype(BF16)
    fetches[0].wait()
    fetches[1].wait()
    kept = []
    for block in range(blocks):
        at = slice(block * BLOCK, (block + 1) * BLOCK)
        fetches[2 + block].wait()
        held = jnp.dot(tokens_ref[at], weight_ref[...], preferred_element_type=F32).astype(BF16)
        pair_ref[at] = held
        kept.append(held)
        mean = jnp.dot(share, held, preferred_element_type=F32)
        mid_ref[block * runs : (block + 1) * runs] = mean[:runs].astype(BF16)
        coarse_ref[block : block + 1] = mean[runs : runs + 1].astype(BF16)
    inner_ref[...] = jnp.where(even, kept[-1], kept[0])
    outer_ref[...] = jnp.where(even, kept[0], kept[-1])


def put_keys(keys_ref, rows, at, biases):
    count = rows.shape[0]
    lane = lax.broadcasted_iota(jnp.int32, (count, HEAD_DIM), 1)
    extra = jnp.zeros((count, HEAD_DIM), F32)
    for order, bias in enumerate(biases):
        extra = jnp.where(lane == order, bias, extra)
    extra = extra.astype(BF16)
    for head in range(KV_HEADS):
        keys_ref[head, pl.ds(at, count), :HEAD_DIM] = rows[:, head * HEAD_DIM : (head + 1) * HEAD_DIM]
        keys_ref[head, pl.ds(at, count), HEAD_DIM:] = extra


def put_values(values_ref, rows):
    width = KV_HEADS * HEAD_DIM
    count = rows.shape[0]
    tall = KV_HEADS * VROWS
    row = lax.broadcasted_iota(jnp.int32, (tall, width), 0)
    column = lax.broadcasted_iota(jnp.int32, (tall, width), 1)
    head, inner = column // HEAD_DIM, column % HEAD_DIM
    pick = jnp.where(row == head * VROWS + inner, 1.0, 0.0).astype(BF16)
    turned = lax.dot_general(pick, rows, NT, preferred_element_type=F32)
    counting = lax.broadcasted_iota(jnp.int32, (tall, count), 0) % VROWS == HEAD_DIM
    values_ref[...] = jnp.where(counting, 1.0, turned).astype(BF16).reshape(KV_HEADS, VROWS, count)


def run_units(before, scores, finish, values, buffers):
    def first(group, block):
        held, top = buffers[block]
        x, floor = scores(group, block)
        held[...] = x
        highest = jnp.max(x, axis=0, keepdims=True)
        top[...] = highest if floor is None else jnp.maximum(highest, floor)

    def second(group, block):
        held, top = buffers[block]
        highest = top[...]
        weights = jnp.exp(held[...] - highest).astype(BF16)
        finish(group, block, highest, jnp.dot(values(group, block), weights, preferred_element_type=F32))

    before(0)
    first(0, 0)

    def step(group, carry):
        before(group + 1)
        first(group, 1)
        second(group, 0)
        first(group + 1, 0)
        second(group, 1)
        return carry

    lax.fori_loop(0, KV_HEADS - 1, step, 0)
    last = KV_HEADS - 1
    first(last, 1)
    second(last, 0)
    second(last, 1)


def near(tokens_ref, wq_hbm, pair_ref, inner_ref, outer_ref, q_hbm, acc_hbm, top_hbm,
         wq_ref, q_ref, acc_ref, top_ref, sems, keys_ref, values_ref, sa, ta, sb, tb):
    rows = tokens_ref.shape[0]
    blocks = rows // BLOCK
    width = KV_HEADS * HEAD_DIM
    span = SHARE * HEAD_DIM
    me = lax.axis_index("seq")
    devices = lax.axis_size("seq")
    even = me % 2 == 0
    fetches = [
        pltpu.make_async_copy(wq_hbm.at[:, pl.ds(group * span, span)], wq_ref.at[group], sems.at[group])
        for group in range(KV_HEADS)
    ]
    for fetch in fetches:
        fetch.start()
    prev = jnp.where(even, outer_ref[...], inner_ref[...])
    follow = jnp.where(even, inner_ref[...], outer_ref[...])
    put_keys(keys_ref, prev[:, :width], 0, [jnp.where(me > 0, 0.0, MASKED)] * blocks)
    put_keys(keys_ref, pair_ref[:, :width], BLOCK, ())
    put_keys(keys_ref, follow[:, :width], BLOCK + rows, [jnp.where(me < devices - 1, 0.0, MASKED)] * blocks)
    put_values(values_ref, jnp.concatenate([prev[:, width:], pair_ref[:, width:], follow[:, width:]], axis=0))
    lane = lax.broadcasted_iota(jnp.int32, (BLOCK, HEAD_DIM), 1)

    def keep(group, source, target, order):
        return pltpu.make_async_copy(source.at[group], target.at[group], sems.at[order * KV_HEADS + group])

    def before(group):
        pltpu.make_async_copy(wq_hbm.at[:, pl.ds(0, span)], wq_ref.at[group], sems.at[group]).wait()
        part = jnp.dot(tokens_ref[...], wq_ref[group], preferred_element_type=F32)
        part = part.astype(BF16) * (1.0 / math.sqrt(HEAD_DIM))
        for block in range(blocks):
            extra = jnp.where(lane == block, 1.0, 0.0).astype(BF16)
            for head in range(SHARE):
                to = slice(head * BLOCK, (head + 1) * BLOCK)
                piece = part[block * BLOCK : (block + 1) * BLOCK, head * HEAD_DIM : (head + 1) * HEAD_DIM]
                q_ref[group, block, to, :HEAD_DIM] = piece
                q_ref[group, block, to, HEAD_DIM:] = extra
        keep(group, q_ref, q_hbm, 1).start()

    def scores(group, block):
        at = slice(block * BLOCK, block * BLOCK + BLOCK + rows)
        return lax.dot_general(keys_ref[group, at], q_ref[group, block], NT, preferred_element_type=F32), None

    def finish(group, block, highest, total):
        acc_ref[group, block] = total
        top_ref[group, block] = highest
        if block == blocks - 1:
            keep(group, acc_ref, acc_hbm, 2).start()

    def values(group, block):
        return values_ref[group, :, block * BLOCK : block * BLOCK + BLOCK + rows]

    run_units(before, scores, finish, values, ((sa, ta), (sb, tb)))
    keep_top = pltpu.make_async_copy(top_ref, top_hbm, sems.at[3 * KV_HEADS])
    keep_top.start()
    for group in range(KV_HEADS):
        keep(group, q_ref, q_hbm, 1).wait()
        keep(group, acc_ref, acc_hbm, 2).wait()
    keep_top.wait()


def far(q_hbm, acc_hbm, top_hbm, mids_ref, coarse_ref, wout_hbm, out_hbm,
        q_ref, acc_ref, top_ref, wout_ref, out_ref, sems, rows_ref, keys_ref, values_ref, mixed_ref, sa, ta, sb, tb):
    def fetch(group, source, target, order):
        return pltpu.make_async_copy(source.at[group], target.at[group], sems.at[order * KV_HEADS + group])

    fetch_top = pltpu.make_async_copy(top_hbm, top_ref, sems.at[2 * KV_HEADS])
    fetch_wout = pltpu.make_async_copy(wout_hbm, wout_ref, sems.at[2 * KV_HEADS + 1])
    fetch_top.start()
    for group in range(KV_HEADS):
        fetch(group, q_hbm, q_ref, 0).start()
        fetch(group, acc_hbm, acc_ref, 1).start()
    fetch_wout.start()
    blocks = mixed_ref.shape[0]
    width = KV_HEADS * HEAD_DIM
    me = lax.axis_index("seq")
    groups = lax.axis_size("seq") // GROUP
    mine = me % GROUP
    runs = BLOCK // POOL
    per_device = runs * blocks
    mid_rows = GROUP * per_device
    spread = blocks * (groups - 1)
    swapped = pl.multiple_of(mine * per_device, per_device)
    for member in range(GROUP):
        rows_ref[member * per_device : (member + 1) * per_device] = mids_ref[member, :per_device]
    rows_ref[pl.ds(swapped, per_device)] = coarse_ref[:per_device]
    if coarse_ref.shape[0] > per_device:
        rows_ref[mid_rows:] = coarse_ref[per_device:]
    indices = [me * blocks + block for block in range(blocks)]
    row = lax.broadcasted_iota(jnp.int32, (mid_rows, HEAD_DIM), 0)
    mid_block = (me - mine + row // per_device) * blocks + row % per_device // runs
    put_keys(keys_ref, rows_ref[:mid_rows, :width], 0, [jnp.where(jnp.abs(mid_block - index) > 1, 0.0, MASKED) for index in indices])
    for start in range(0, coarse_ref.shape[0], per_device):
        row = lax.broadcasted_iota(jnp.int32, (per_device, HEAD_DIM), 0) + start
        other = (row % spread) // blocks + 1
        far_block = (((me // GROUP) ^ other) * GROUP + row // spread) * blocks + row % blocks
        bias = [jnp.where(jnp.abs(far_block - index) > 1, 0.0, MASKED) for index in indices]
        at = swapped if start == 0 else mid_rows + start - per_device
        put_keys(keys_ref, coarse_ref[start : start + per_device, :width], at, bias)
    put_values(values_ref, rows_ref[:, width:])
    fetch_top.wait()

    def before(group):
        fetch(group, q_hbm, q_ref, 0).wait()
        fetch(group, acc_hbm, acc_ref, 1).wait()

    def scores(group, block):
        return lax.dot_general(keys_ref[group], q_ref[group, block], NT, preferred_element_type=F32), top_ref[group, block]

    def finish(group, block, highest, total):
        total = total + acc_ref[group, block] * jnp.exp(top_ref[group, block] - highest)
        share = total[:HEAD_DIM] / total[HEAD_DIM : HEAD_DIM + 1]
        share = share.astype(BF16)
        for head in range(SHARE):
            to = pl.multiple_of((group * SHARE + head) * HEAD_DIM, HEAD_DIM)
            mixed_ref[block, pl.ds(to, HEAD_DIM), :] = share[:, head * BLOCK : (head + 1) * BLOCK]

    run_units(before, scores, finish, lambda group, block: values_ref[group], ((sa, ta), (sb, tb)))
    fetch_wout.wait()
    stores = []
    for block in range(blocks):
        at = pl.ds(block * BLOCK, BLOCK)
        out_ref[at] = lax.dot_general(mixed_ref[block], wout_ref[...], TN, preferred_element_type=F32).astype(BF16)
        store = pltpu.make_async_copy(out_ref.at[at], out_hbm.at[at], sems.at[2 * KV_HEADS + 2 + block])
        store.start()
        stores.append(store)
    for store in stores:
        store.wait()


def body(tokens, w_query, w_key, w_value, w_out):
    devices = lax.axis_size("seq")
    rows, model = tokens.shape
    blocks = rows // BLOCK
    width = KV_HEADS * HEAD_DIM
    stack = SHARE * BLOCK
    per_device = rows // POOL
    shape = jax.ShapeDtypeStruct
    dma = pltpu.SemaphoreType.DMA

    def call(kernel, out_shape, in_specs, out_specs, scratch, flops, name, kib=53000):
        return pl.pallas_call(
            kernel,
            out_shape=out_shape,
            in_specs=in_specs,
            out_specs=out_specs,
            scratch_shapes=scratch,
            compiler_params=pltpu.CompilerParams(vmem_limit_bytes=kib * 2**10),
            cost_estimate=pl.CostEstimate(flops=flops, bytes_accessed=2**20, transcendentals=0),
            name=name,
        )

    def slots(keys):
        return [pltpu.VMEM((keys, stack), F32), pltpu.VMEM((1, stack), F32)] * 2

    half = shape((BLOCK, 2 * width), BF16)
    pair, mid, coarse, inner, outer = call(
        project_pair,
        [shape((rows, 2 * width), BF16), shape((per_device, 2 * width), BF16), shape((blocks, 2 * width), BF16), half, half],
        [HBM] * 3,
        [VMEM] * 5,
        [pltpu.VMEM((rows, model), BF16), pltpu.VMEM((model, 2 * width), BF16), dma((2 + blocks,))],
        2 * 10**9,
        "pair",
        54000,
    )(tokens, w_key, w_value)

    state = [shape((KV_HEADS, blocks, stack, WIDE), BF16), shape((KV_HEADS, blocks, VROWS, stack), F32), shape((KV_HEADS, blocks, 1, stack), F32)]
    held = [pltpu.VMEM(part.shape, part.dtype) for part in state]
    spread = coarse
    level = GROUP
    while level < devices:
        spread = jnp.concatenate([spread, swap(spread, level)], axis=0)
        level *= 2
    spread = spread[blocks:]
    inner = swap(inner, 1)
    links = [(i, i + 1) for i in range(1, devices - 1, 2)]
    outer = lax.ppermute(tied(outer, spread), "seq", links + [(b, a) for a, b in links])
    payload = jnp.concatenate([mid, spread], axis=0)
    payload = jnp.broadcast_to(payload[None], (GROUP, *payload.shape))
    members = [list(range(at, at + GROUP)) for at in range(0, devices, GROUP)]
    arrived = lax.all_to_all(payload, "seq", 0, 0, axis_index_groups=members)

    q, acc, top = call(
        near,
        state,
        [VMEM, HBM, VMEM, VMEM, VMEM],
        [HBM] * 3,
        [pltpu.VMEM((KV_HEADS, model, SHARE * HEAD_DIM), BF16)]
        + held
        + [dma((3 * KV_HEADS + 1,)), pltpu.VMEM((KV_HEADS, rows + 2 * BLOCK, WIDE), BF16), pltpu.VMEM((KV_HEADS, VROWS, rows + 2 * BLOCK), BF16)]
        + slots(rows + BLOCK),
        10**10,
        "near",
    )(tokens, w_query, tied(pair, payload), inner, outer)

    coarse_far = arrived[:, per_device:].reshape(-1, 2 * width)
    keys = (GROUP - 1) * per_device + coarse_far.shape[0]
    return call(
        far,
        shape((rows, w_out.shape[1]), BF16),
        [HBM] * 3 + [VMEM, VMEM, HBM],
        HBM,
        held
        + [
            pltpu.VMEM(w_out.shape, BF16),
            pltpu.VMEM((rows, w_out.shape[1]), BF16),
            dma((2 * KV_HEADS + 2 + blocks,)),
            pltpu.VMEM((keys, 2 * width), BF16),
            pltpu.VMEM((KV_HEADS, keys, WIDE), BF16),
            pltpu.VMEM((KV_HEADS, VROWS, keys), BF16),
            pltpu.VMEM((blocks, HEADS * HEAD_DIM, BLOCK), BF16),
        ]
        + slots(keys),
        8 * 10**9,
        "far",
    )(q, acc, top, arrived, coarse_far, w_out)


def solution(mesh):
    placed = (P("seq", None), P(), P(), P(), P())
    return jax.shard_map(body, mesh=mesh, in_specs=placed, out_specs=P("seq", None), check_vma=False)
```

```python
import math

import jax
import jax.numpy as jnp
from jax import lax
from jax.experimental import pallas as pl
from jax.experimental.pallas import tpu as pltpu
from jax.sharding import PartitionSpec as P

HEADS = 16
KV_HEADS = 4
HEAD_DIM = 64
BLOCK = 256
POOL = 16
GROUP = 16
SHARE = HEADS // KV_HEADS
WIDE = 128
VROWS = 80
BF16 = jnp.bfloat16
F32 = jnp.float32
NT = (((1,), (1,)), ((), ()))
TN = (((0,), (0,)), ((), ()))
MASKED = -1e30
VMEM = pl.BlockSpec(memory_space=pltpu.VMEM)
HBM = pl.BlockSpec(memory_space=pltpu.HBM)


def swap(rows, apart):
    count = lax.axis_size("seq")
    return lax.ppermute(rows, "seq", [(i, i ^ apart) for i in range(count)])


def tied(rows, *others):
    return lax.optimization_barrier((rows, *others))[0]


def project_pair(tokens_hbm, wk_hbm, wv_hbm, pair_ref, mid_ref, coarse_ref, inner_ref, outer_ref, tokens_ref, weight_ref, sems):
    rows = tokens_ref.shape[0]
    width = wk_hbm.shape[1]
    blocks = rows // BLOCK
    fetches = [pltpu.make_async_copy(wk_hbm, weight_ref.at[:, pl.ds(0, width)], sems.at[0])]
    fetches.append(pltpu.make_async_copy(wv_hbm, weight_ref.at[:, pl.ds(width, width)], sems.at[1]))
    for block in range(blocks):
        at = pl.ds(block * BLOCK, BLOCK)
        fetches.append(pltpu.make_async_copy(tokens_hbm.at[at], tokens_ref.at[at], sems.at[2 + block]))
    for fetch in fetches:
        fetch.start()
    even = lax.axis_index("seq") % 2 == 0
    runs = BLOCK // POOL
    tall = 3 * runs // 2
    row = lax.broadcasted_iota(jnp.int32, (tall, BLOCK), 0)
    column = lax.broadcasted_iota(jnp.int32, (tall, BLOCK), 1)
    share = jnp.where(row < runs, jnp.where(column // POOL == row, 1.0 / POOL, 0.0), jnp.where(row == runs, 1.0 / BLOCK, 0.0))
    share = share.astype(BF16)
    fetches[0].wait()
    fetches[1].wait()
    kept = []
    for block in range(blocks):
        at = slice(block * BLOCK, (block + 1) * BLOCK)
        fetches[2 + block].wait()
        held = jnp.dot(tokens_ref[at], weight_ref[...], preferred_element_type=F32).astype(BF16)
        pair_ref[at] = held
        kept.append(held)
        mean = jnp.dot(share, held, preferred_element_type=F32)
        mid_ref[block * runs : (block + 1) * runs] = mean[:runs].astype(BF16)
        coarse_ref[block : block + 1] = mean[runs : runs + 1].astype(BF16)
    inner_ref[...] = jnp.where(even, kept[-1], kept[0])
    outer_ref[...] = jnp.where(even, kept[0], kept[-1])


def put_keys(keys_ref, rows, at, biases):
    count = rows.shape[0]
    lane = lax.broadcasted_iota(jnp.int32, (count, HEAD_DIM), 1)
    extra = jnp.zeros((count, HEAD_DIM), F32)
    for order, bias in enumerate(biases):
        extra = jnp.where(lane == order, bias, extra)
    extra = extra.astype(BF16)
    for head in range(KV_HEADS):
        keys_ref[head, pl.ds(at, count), :HEAD_DIM] = rows[:, head * HEAD_DIM : (head + 1) * HEAD_DIM]
        keys_ref[head, pl.ds(at, count), HEAD_DIM:] = extra


def put_values(values_ref, rows):
    width = KV_HEADS * HEAD_DIM
    count = rows.shape[0]
    tall = KV_HEADS * VROWS
    row = lax.broadcasted_iota(jnp.int32, (tall, width), 0)
    column = lax.broadcasted_iota(jnp.int32, (tall, width), 1)
    head, inner = column // HEAD_DIM, column % HEAD_DIM
    pick = jnp.where(row == head * VROWS + inner, 1.0, 0.0).astype(BF16)
    turned = lax.dot_general(pick, rows, NT, preferred_element_type=F32)
    counting = lax.broadcasted_iota(jnp.int32, (tall, count), 0) % VROWS == HEAD_DIM
    values_ref[...] = jnp.where(counting, 1.0, turned).astype(BF16).reshape(KV_HEADS, VROWS, count)


def run_units(before, scores, finish, values, buffers, closing=None, between=None):
    def first(group, block):
        held, top = buffers[block]
        x, floor = scores(group, block)
        held[...] = x
        highest = jnp.max(x, axis=0, keepdims=True)
        top[...] = highest if floor is None else jnp.maximum(highest, floor)

    def second(group, block):
        held, top = buffers[block]
        highest = top[...]
        weights = jnp.exp(held[...] - highest).astype(BF16)
        finish(group, block, highest, jnp.dot(values(group, block), weights, preferred_element_type=F32))

    before(0)
    first(0, 0)

    def step(group, carry):
        before(group + 1)
        first(group, 1)
        second(group, 0)
        first(group + 1, 0)
        second(group, 1)
        return carry

    lax.fori_loop(0, KV_HEADS - 1, step, 0)
    if closing is not None:
        closing()
    last = KV_HEADS - 1
    first(last, 1)
    second(last, 0)
    if between is not None:
        between()
    second(last, 1)


def near(tokens_ref, wq_hbm, pair_ref, inner_ref, outer_ref, q_hbm, acc_hbm, top_hbm,
         wq_ref, q_ref, acc_ref, top_ref, sems, keys_ref, values_ref, sa, ta, sb, tb):
    rows = tokens_ref.shape[0]
    blocks = rows // BLOCK
    width = KV_HEADS * HEAD_DIM
    span = SHARE * HEAD_DIM
    me = lax.axis_index("seq")
    devices = lax.axis_size("seq")
    even = me % 2 == 0
    fetches = [
        pltpu.make_async_copy(wq_hbm.at[:, pl.ds(group * span, span)], wq_ref.at[group], sems.at[group])
        for group in range(KV_HEADS)
    ]
    for fetch in fetches:
        fetch.start()
    prev = jnp.where(even, outer_ref[...], inner_ref[...])
    follow = jnp.where(even, inner_ref[...], outer_ref[...])
    put_keys(keys_ref, prev[:, :width], 0, [jnp.where(me > 0, 0.0, MASKED)] * blocks)
    put_keys(keys_ref, pair_ref[:, :width], BLOCK, ())
    put_keys(keys_ref, follow[:, :width], BLOCK + rows, [jnp.where(me < devices - 1, 0.0, MASKED)] * blocks)
    put_values(values_ref, jnp.concatenate([prev[:, width:], pair_ref[:, width:], follow[:, width:]], axis=0))
    lane = lax.broadcasted_iota(jnp.int32, (BLOCK, HEAD_DIM), 1)

    def keep(group, source, target, order):
        return pltpu.make_async_copy(source.at[group], target.at[group], sems.at[order * KV_HEADS + group])

    def leave(group, block):
        return pltpu.make_async_copy(acc_ref.at[group, block], acc_hbm.at[group, block], sems.at[2 * KV_HEADS + 1 + group * blocks + block])

    def send(group):
        for block in range(blocks):
            leave(group, block).start()

    def before(group):
        pltpu.make_async_copy(wq_hbm.at[:, pl.ds(0, span)], wq_ref.at[group], sems.at[group]).wait()

        @pl.when(group >= 1)
        def _():
            keep(group - 1, q_ref, q_hbm, 1).start()

        @pl.when(group >= 2)
        def _():
            send(group - 2)

        part = jnp.dot(tokens_ref[...], wq_ref[group], preferred_element_type=F32)
        part = part.astype(BF16) * (1.0 / math.sqrt(HEAD_DIM))
        for block in range(blocks):
            extra = jnp.where(lane == block, 1.0, 0.0).astype(BF16)
            for head in range(SHARE):
                to = slice(head * BLOCK, (head + 1) * BLOCK)
                piece = part[block * BLOCK : (block + 1) * BLOCK, head * HEAD_DIM : (head + 1) * HEAD_DIM]
                q_ref[group, block, to, :HEAD_DIM] = piece
                q_ref[group, block, to, HEAD_DIM:] = extra

    def closing():
        keep(KV_HEADS - 1, q_ref, q_hbm, 1).start()
        send(KV_HEADS - 2)

    def scores(group, block):
        at = slice(block * BLOCK, block * BLOCK + BLOCK + rows)
        return lax.dot_general(keys_ref[group, at], q_ref[group, block], NT, preferred_element_type=F32), None

    def finish(group, block, highest, total):
        acc_ref[group, block] = total
        top_ref[group, block] = highest

    def values(group, block):
        return values_ref[group, :, block * BLOCK : block * BLOCK + BLOCK + rows]

    run_units(before, scores, finish, values, ((sa, ta), (sb, tb)), closing)
    send(KV_HEADS - 1)
    keep_top = pltpu.make_async_copy(top_ref, top_hbm, sems.at[2 * KV_HEADS])
    keep_top.start()
    for group in range(KV_HEADS):
        keep(group, q_ref, q_hbm, 1).wait()
        for block in range(blocks):
            leave(group, block).wait()
    keep_top.wait()


def far(q_hbm, acc_hbm, top_hbm, mids_ref, coarse_ref, wout_hbm, out_hbm,
        q_ref, acc_ref, top_ref, wout_ref, out_ref, sems, rows_ref, keys_ref, values_ref, mixed_ref, sa, ta, sb, tb):
    def fetch(group, source, target, order):
        return pltpu.make_async_copy(source.at[group], target.at[group], sems.at[order * KV_HEADS + group])

    fetch_top = pltpu.make_async_copy(top_hbm, top_ref, sems.at[2 * KV_HEADS])
    fetch_wout = pltpu.make_async_copy(wout_hbm, wout_ref, sems.at[2 * KV_HEADS + 1])
    fetch_top.start()
    for group in range(KV_HEADS):
        fetch(group, q_hbm, q_ref, 0).start()
        fetch(group, acc_hbm, acc_ref, 1).start()
    fetch_wout.start()
    blocks = mixed_ref.shape[0]
    width = KV_HEADS * HEAD_DIM
    me = lax.axis_index("seq")
    groups = lax.axis_size("seq") // GROUP
    mine = me % GROUP
    runs = BLOCK // POOL
    per_device = runs * blocks
    mid_rows = GROUP * per_device
    spread = blocks * (groups - 1)
    swapped = pl.multiple_of(mine * per_device, per_device)
    for member in range(GROUP):
        rows_ref[member * per_device : (member + 1) * per_device] = mids_ref[member, :per_device]
    rows_ref[pl.ds(swapped, per_device)] = coarse_ref[:per_device]
    if coarse_ref.shape[0] > per_device:
        rows_ref[mid_rows:] = coarse_ref[per_device:]
    indices = [me * blocks + block for block in range(blocks)]
    row = lax.broadcasted_iota(jnp.int32, (mid_rows, HEAD_DIM), 0)
    mid_block = (me - mine + row // per_device) * blocks + row % per_device // runs
    put_keys(keys_ref, rows_ref[:mid_rows, :width], 0, [jnp.where(jnp.abs(mid_block - index) > 1, 0.0, MASKED) for index in indices])
    for start in range(0, coarse_ref.shape[0], per_device):
        row = lax.broadcasted_iota(jnp.int32, (per_device, HEAD_DIM), 0) + start
        other = (row % spread) // blocks + 1
        far_block = (((me // GROUP) ^ other) * GROUP + row // spread) * blocks + row % blocks
        bias = [jnp.where(jnp.abs(far_block - index) > 1, 0.0, MASKED) for index in indices]
        at = swapped if start == 0 else mid_rows + start - per_device
        put_keys(keys_ref, coarse_ref[start : start + per_device, :width], at, bias)
    put_values(values_ref, rows_ref[:, width:])
    fetch_top.wait()

    def before(group):
        fetch(group, q_hbm, q_ref, 0).wait()
        fetch(group, acc_hbm, acc_ref, 1).wait()

    def scores(group, block):
        return lax.dot_general(keys_ref[group], q_ref[group, block], NT, preferred_element_type=F32), top_ref[group, block]

    def finish(group, block, highest, total):
        total = total + acc_ref[group, block] * jnp.exp(top_ref[group, block] - highest)
        share = total[:HEAD_DIM] / total[HEAD_DIM : HEAD_DIM + 1]
        share = share.astype(BF16)
        for head in range(SHARE):
            to = pl.multiple_of((group * SHARE + head) * HEAD_DIM, HEAD_DIM)
            mixed_ref[block, pl.ds(to, HEAD_DIM), :] = share[:, head * BLOCK : (head + 1) * BLOCK]

    def store(block):
        at = pl.ds(block * BLOCK, BLOCK)
        return pltpu.make_async_copy(out_ref.at[at], out_hbm.at[at], sems.at[2 * KV_HEADS + 2 + block])

    def project(block):
        at = pl.ds(block * BLOCK, BLOCK)
        out_ref[at] = lax.dot_general(mixed_ref[block], wout_ref[...], TN, preferred_element_type=F32).astype(BF16)

    run_units(before, scores, finish, lambda group, block: values_ref[group], ((sa, ta), (sb, tb)), fetch_wout.wait, lambda: project(0))
    store(0).start()
    for block in range(1, blocks):
        project(block)
        store(block).start()
    for block in range(blocks):
        store(block).wait()


def body(tokens, w_query, w_key, w_value, w_out):
    devices = lax.axis_size("seq")
    rows, model = tokens.shape
    blocks = rows // BLOCK
    width = KV_HEADS * HEAD_DIM
    stack = SHARE * BLOCK
    per_device = rows // POOL
    shape = jax.ShapeDtypeStruct
    dma = pltpu.SemaphoreType.DMA

    def call(kernel, out_shape, in_specs, out_specs, scratch, flops, name, kib=53000):
        return pl.pallas_call(
            kernel,
            out_shape=out_shape,
            in_specs=in_specs,
            out_specs=out_specs,
            scratch_shapes=scratch,
            compiler_params=pltpu.CompilerParams(vmem_limit_bytes=kib * 2**10),
            cost_estimate=pl.CostEstimate(flops=flops, bytes_accessed=2**20, transcendentals=0),
            name=name,
        )

    def slots(keys):
        return [pltpu.VMEM((keys, stack), F32), pltpu.VMEM((1, stack), F32)] * 2

    half = shape((BLOCK, 2 * width), BF16)
    pair, mid, coarse, inner, outer = call(
        project_pair,
        [shape((rows, 2 * width), BF16), shape((per_device, 2 * width), BF16), shape((blocks, 2 * width), BF16), half, half],
        [HBM] * 3,
        [VMEM] * 5,
        [pltpu.VMEM((rows, model), BF16), pltpu.VMEM((model, 2 * width), BF16), dma((2 + blocks,))],
        2 * 10**9,
        "pair",
        54000,
    )(tokens, w_key, w_value)

    state = [shape((KV_HEADS, blocks, stack, WIDE), BF16), shape((KV_HEADS, blocks, VROWS, stack), F32), shape((KV_HEADS, blocks, 1, stack), F32)]
    held = [pltpu.VMEM(part.shape, part.dtype) for part in state]
    spread = coarse
    level = GROUP
    while level < devices:
        spread = jnp.concatenate([spread, swap(spread, level)], axis=0)
        level *= 2
    spread = spread[blocks:]
    inner = swap(inner, 1)
    links = [(i, i + 1) for i in range(1, devices - 1, 2)]
    outer = lax.ppermute(tied(outer, spread), "seq", links + [(b, a) for a, b in links])
    payload = jnp.concatenate([mid, spread], axis=0)
    payload = jnp.broadcast_to(payload[None], (GROUP, *payload.shape))
    members = [list(range(at, at + GROUP)) for at in range(0, devices, GROUP)]
    arrived = lax.all_to_all(payload, "seq", 0, 0, axis_index_groups=members)

    q, acc, top = call(
        near,
        state,
        [VMEM, HBM, VMEM, VMEM, VMEM],
        [HBM] * 3,
        [pltpu.VMEM((KV_HEADS, model, SHARE * HEAD_DIM), BF16)]
        + held
        + [dma((2 * KV_HEADS + 1 + KV_HEADS * blocks,)), pltpu.VMEM((KV_HEADS, rows + 2 * BLOCK, WIDE), BF16), pltpu.VMEM((KV_HEADS, VROWS, rows + 2 * BLOCK), BF16)]
        + slots(rows + BLOCK),
        10**10,
        "near",
    )(tokens, w_query, tied(pair, payload), inner, outer)

    coarse_far = arrived[:, per_device:].reshape(-1, 2 * width)
    keys = (GROUP - 1) * per_device + coarse_far.shape[0]
    return call(
        far,
        shape((rows, w_out.shape[1]), BF16),
        [HBM] * 3 + [VMEM, VMEM, HBM],
        HBM,
        held
        + [
            pltpu.VMEM(w_out.shape, BF16),
            pltpu.VMEM((rows, w_out.shape[1]), BF16),
            dma((2 * KV_HEADS + 2 + blocks,)),
            pltpu.VMEM((keys, 2 * width), BF16),
            pltpu.VMEM((KV_HEADS, keys, WIDE), BF16),
            pltpu.VMEM((KV_HEADS, VROWS, keys), BF16),
            pltpu.VMEM((blocks, HEADS * HEAD_DIM, BLOCK), BF16),
        ]
        + slots(keys),
        8 * 10**9,
        "far",
    )(q, acc, top, arrived, coarse_far, w_out)


def solution(mesh):
    placed = (P("seq", None), P(), P(), P(), P())
    return jax.shard_map(body, mesh=mesh, in_specs=placed, out_specs=P("seq", None), check_vma=False)
```

```python
import math

import jax
import jax.numpy as jnp
from jax import lax
from jax.experimental import pallas as pl
from jax.experimental.pallas import tpu as pltpu
from jax.sharding import PartitionSpec as P

HEADS = 16
KV_HEADS = 4
HEAD_DIM = 64
BLOCK = 256
POOL = 16
GROUP = 16
SHARE = HEADS // KV_HEADS
WIDE = 128
VROWS = 80
BF16 = jnp.bfloat16
F32 = jnp.float32
NT = (((1,), (1,)), ((), ()))
TN = (((0,), (0,)), ((), ()))
MASKED = -1e30
VMEM = pl.BlockSpec(memory_space=pltpu.VMEM)
HBM = pl.BlockSpec(memory_space=pltpu.HBM)


def swap(rows, apart):
    count = lax.axis_size("seq")
    return lax.ppermute(rows, "seq", [(i, i ^ apart) for i in range(count)])


def tied(rows, *others):
    return lax.optimization_barrier((rows, *others))[0]


def project_pair(tokens_hbm, wk_hbm, wv_hbm, pair_ref, mid_ref, coarse_ref, inner_ref, outer_ref, tokens_ref, weight_ref, sems):
    rows = tokens_ref.shape[0]
    width = wk_hbm.shape[1]
    blocks = rows // BLOCK
    fetches = [pltpu.make_async_copy(wk_hbm, weight_ref.at[:, pl.ds(0, width)], sems.at[0])]
    fetches.append(pltpu.make_async_copy(wv_hbm, weight_ref.at[:, pl.ds(width, width)], sems.at[1]))
    for block in range(blocks):
        at = pl.ds(block * BLOCK, BLOCK)
        fetches.append(pltpu.make_async_copy(tokens_hbm.at[at], tokens_ref.at[at], sems.at[2 + block]))
    for fetch in fetches:
        fetch.start()
    even = lax.axis_index("seq") % 2 == 0
    runs = BLOCK // POOL
    tall = 3 * runs // 2
    row = lax.broadcasted_iota(jnp.int32, (tall, BLOCK), 0)
    column = lax.broadcasted_iota(jnp.int32, (tall, BLOCK), 1)
    share = jnp.where(row < runs, jnp.where(column // POOL == row, 1.0 / POOL, 0.0), jnp.where(row == runs, 1.0 / BLOCK, 0.0))
    share = share.astype(BF16)
    fetches[0].wait()
    fetches[1].wait()
    kept = []
    for block in range(blocks):
        at = slice(block * BLOCK, (block + 1) * BLOCK)
        fetches[2 + block].wait()
        held = jnp.dot(tokens_ref[at], weight_ref[...], preferred_element_type=F32).astype(BF16)
        pair_ref[at] = held
        kept.append(held)
        mean = jnp.dot(share, held, preferred_element_type=F32)
        mid_ref[block * runs : (block + 1) * runs] = mean[:runs].astype(BF16)
        coarse_ref[block : block + 1] = mean[runs : runs + 1].astype(BF16)
    inner_ref[...] = jnp.where(even, kept[-1], kept[0])
    outer_ref[...] = jnp.where(even, kept[0], kept[-1])


def put_keys(keys_ref, rows, at, biases):
    count = rows.shape[0]
    lane = lax.broadcasted_iota(jnp.int32, (count, HEAD_DIM), 1)
    extra = jnp.zeros((count, HEAD_DIM), F32)
    for order, bias in enumerate(biases):
        extra = jnp.where(lane == order, bias, extra)
    extra = extra.astype(BF16)
    for head in range(KV_HEADS):
        keys_ref[head, pl.ds(at, count), :HEAD_DIM] = rows[:, head * HEAD_DIM : (head + 1) * HEAD_DIM]
        keys_ref[head, pl.ds(at, count), HEAD_DIM:] = extra


def put_values(values_ref, rows):
    width = KV_HEADS * HEAD_DIM
    count = rows.shape[0]
    tall = KV_HEADS * VROWS
    row = lax.broadcasted_iota(jnp.int32, (tall, width), 0)
    column = lax.broadcasted_iota(jnp.int32, (tall, width), 1)
    head, inner = column // HEAD_DIM, column % HEAD_DIM
    pick = jnp.where(row == head * VROWS + inner, 1.0, 0.0).astype(BF16)
    turned = lax.dot_general(pick, rows, NT, preferred_element_type=F32)
    counting = lax.broadcasted_iota(jnp.int32, (tall, count), 0) % VROWS == HEAD_DIM
    values_ref[...] = jnp.where(counting, 1.0, turned).astype(BF16).reshape(KV_HEADS, VROWS, count)


def run_units(before, scores, finish, values, buffers, closing=None, between=None):
    def first(group, block):
        held, top = buffers[block]
        x, floor = scores(group, block)
        held[...] = x
        highest = jnp.max(x, axis=0, keepdims=True)
        top[...] = highest if floor is None else jnp.maximum(highest, floor)

    def second(group, block):
        held, top = buffers[block]
        highest = top[...]
        weights = jnp.exp(held[...] - highest).astype(BF16)
        finish(group, block, highest, jnp.dot(values(group, block), weights, preferred_element_type=F32))

    before(0)
    first(0, 0)

    def step(group, carry):
        before(group + 1)
        first(group, 1)
        second(group, 0)
        first(group + 1, 0)
        second(group, 1)
        return carry

    lax.fori_loop(0, KV_HEADS - 1, step, 0)
    if closing is not None:
        closing()
    last = KV_HEADS - 1
    first(last, 1)
    second(last, 0)
    if between is not None:
        between()
    second(last, 1)


def near(tokens_ref, wq_hbm, pair_ref, inner_ref, outer_ref, q_hbm, acc_hbm, top_hbm,
         wq_ref, q_ref, acc_ref, top_ref, sems, keys_ref, values_ref, sa, ta, sb, tb):
    rows = tokens_ref.shape[0]
    blocks = rows // BLOCK
    width = KV_HEADS * HEAD_DIM
    span = SHARE * HEAD_DIM
    me = lax.axis_index("seq")
    devices = lax.axis_size("seq")
    even = me % 2 == 0
    fetches = [
        pltpu.make_async_copy(wq_hbm.at[:, pl.ds(group * span, span)], wq_ref.at[group], sems.at[group])
        for group in range(KV_HEADS)
    ]
    for fetch in fetches:
        fetch.start()
    prev = jnp.where(even, outer_ref[...], inner_ref[...])
    follow = jnp.where(even, inner_ref[...], outer_ref[...])
    put_keys(keys_ref, prev[:, :width], 0, [jnp.where(me > 0, 0.0, MASKED)] * blocks)
    put_keys(keys_ref, pair_ref[:, :width], BLOCK, ())
    put_keys(keys_ref, follow[:, :width], BLOCK + rows, [jnp.where(me < devices - 1, 0.0, MASKED)] * blocks)
    put_values(values_ref, jnp.concatenate([prev[:, width:], pair_ref[:, width:], follow[:, width:]], axis=0))
    lane = lax.broadcasted_iota(jnp.int32, (BLOCK, HEAD_DIM), 1)

    def keep(group, source, target, order):
        return pltpu.make_async_copy(source.at[group], target.at[group], sems.at[order * KV_HEADS + group])

    def leave(group, block):
        return pltpu.make_async_copy(acc_ref.at[group, block], acc_hbm.at[group, block], sems.at[2 * KV_HEADS + 1 + group * blocks + block])

    def send(group):
        for block in range(blocks):
            leave(group, block).start()

    def before(group):
        pltpu.make_async_copy(wq_hbm.at[:, pl.ds(0, span)], wq_ref.at[group], sems.at[group]).wait()

        @pl.when(group >= 1)
        def _():
            keep(group - 1, q_ref, q_hbm, 1).start()

        @pl.when(group >= 2)
        def _():
            send(group - 2)

        part = jnp.dot(tokens_ref[...], wq_ref[group], preferred_element_type=F32)
        part = part.astype(BF16) * (1.0 / math.sqrt(HEAD_DIM))
        for block in range(blocks):
            extra = jnp.where(lane == block, 1.0, 0.0).astype(BF16)
            for head in range(SHARE):
                to = slice(head * BLOCK, (head + 1) * BLOCK)
                piece = part[block * BLOCK : (block + 1) * BLOCK, head * HEAD_DIM : (head + 1) * HEAD_DIM]
                q_ref[group, block, to, :HEAD_DIM] = piece
                q_ref[group, block, to, HEAD_DIM:] = extra

    def closing():
        keep(KV_HEADS - 1, q_ref, q_hbm, 1).start()
        send(KV_HEADS - 2)

    def scores(group, block):
        at = slice(block * BLOCK, block * BLOCK + BLOCK + rows)
        return lax.dot_general(keys_ref[group, at], q_ref[group, block], NT, preferred_element_type=F32), None

    def finish(group, block, highest, total):
        acc_ref[group, block] = total
        top_ref[group, block] = highest

    def values(group, block):
        return values_ref[group, :, block * BLOCK : block * BLOCK + BLOCK + rows]

    run_units(before, scores, finish, values, ((sa, ta), (sb, tb)), closing)
    send(KV_HEADS - 1)
    keep_top = pltpu.make_async_copy(top_ref, top_hbm, sems.at[2 * KV_HEADS])
    keep_top.start()
    for group in range(KV_HEADS):
        keep(group, q_ref, q_hbm, 1).wait()
        for block in range(blocks):
            leave(group, block).wait()
    keep_top.wait()


def far(q_hbm, acc_hbm, top_hbm, mids_ref, coarse_ref, wout_hbm, out_hbm,
        q_ref, acc_ref, top_ref, wout_ref, out_ref, sems, rows_ref, keys_ref, values_ref, mixed_ref, sa, ta, sb, tb):
    def fetch(group, source, target, order):
        return pltpu.make_async_copy(source.at[group], target.at[group], sems.at[order * KV_HEADS + group])

    fetch_top = pltpu.make_async_copy(top_hbm, top_ref, sems.at[2 * KV_HEADS])
    fetch_wout = pltpu.make_async_copy(wout_hbm, wout_ref, sems.at[2 * KV_HEADS + 1])
    fetch_top.start()
    for group in range(KV_HEADS):
        fetch(group, q_hbm, q_ref, 0).start()
        fetch(group, acc_hbm, acc_ref, 1).start()
    fetch_wout.start()
    blocks = mixed_ref.shape[0]
    width = KV_HEADS * HEAD_DIM
    me = lax.axis_index("seq")
    groups = lax.axis_size("seq") // GROUP
    mine = me % GROUP
    runs = BLOCK // POOL
    per_device = runs * blocks
    mid_rows = GROUP * per_device
    spread = blocks * (groups - 1)
    swapped = pl.multiple_of(mine * per_device, per_device)
    for member in range(GROUP):
        rows_ref[member * per_device : (member + 1) * per_device] = mids_ref[member, :per_device]
    rows_ref[pl.ds(swapped, per_device)] = coarse_ref[:per_device]
    if coarse_ref.shape[0] > per_device:
        rows_ref[mid_rows:] = coarse_ref[per_device:]
    indices = [me * blocks + block for block in range(blocks)]
    row = lax.broadcasted_iota(jnp.int32, (mid_rows, HEAD_DIM), 0)
    mid_block = (me - mine + row // per_device) * blocks + row % per_device // runs
    put_keys(keys_ref, rows_ref[:mid_rows, :width], 0, [jnp.where(jnp.abs(mid_block - index) > 1, 0.0, MASKED) for index in indices])
    for start in range(0, coarse_ref.shape[0], per_device):
        row = lax.broadcasted_iota(jnp.int32, (per_device, HEAD_DIM), 0) + start
        other = (row % spread) // blocks + 1
        far_block = (((me // GROUP) ^ other) * GROUP + row // spread) * blocks + row % blocks
        bias = [jnp.where(jnp.abs(far_block - index) > 1, 0.0, MASKED) for index in indices]
        at = swapped if start == 0 else mid_rows + start - per_device
        put_keys(keys_ref, coarse_ref[start : start + per_device, :width], at, bias)
    put_values(values_ref, rows_ref[:, width:])
    fetch_top.wait()

    def before(group):
        fetch(group, q_hbm, q_ref, 0).wait()
        fetch(group, acc_hbm, acc_ref, 1).wait()

    def scores(group, block):
        return lax.dot_general(keys_ref[group], q_ref[group, block], NT, preferred_element_type=F32), top_ref[group, block]

    def finish(group, block, highest, total):
        total = total + acc_ref[group, block] * jnp.exp(top_ref[group, block] - highest)
        share = total[:HEAD_DIM] / total[HEAD_DIM : HEAD_DIM + 1]
        share = share.astype(BF16)
        for head in range(SHARE):
            to = pl.multiple_of((group * SHARE + head) * HEAD_DIM, HEAD_DIM)
            mixed_ref[block, pl.ds(to, HEAD_DIM), :] = share[:, head * BLOCK : (head + 1) * BLOCK]

    def store(block):
        at = pl.ds(block * BLOCK, BLOCK)
        return pltpu.make_async_copy(out_ref.at[at], out_hbm.at[at], sems.at[2 * KV_HEADS + 2 + block])

    def project(block):
        at = pl.ds(block * BLOCK, BLOCK)
        out_ref[at] = lax.dot_general(mixed_ref[block], wout_ref[...], TN, preferred_element_type=F32).astype(BF16)

    run_units(before, scores, finish, lambda group, block: values_ref[group], ((sa, ta), (sb, tb)), fetch_wout.wait, lambda: project(0))
    store(0).start()
    for block in range(1, blocks):
        project(block)
        store(block).start()
    for block in range(blocks):
        store(block).wait()


def body(tokens, w_query, w_key, w_value, w_out):
    devices = lax.axis_size("seq")
    rows, model = tokens.shape
    blocks = rows // BLOCK
    width = KV_HEADS * HEAD_DIM
    stack = SHARE * BLOCK
    per_device = rows // POOL
    shape = jax.ShapeDtypeStruct
    dma = pltpu.SemaphoreType.DMA

    def call(kernel, out_shape, in_specs, out_specs, scratch, flops, name, kib=53000):
        return pl.pallas_call(
            kernel,
            out_shape=out_shape,
            in_specs=in_specs,
            out_specs=out_specs,
            scratch_shapes=scratch,
            compiler_params=pltpu.CompilerParams(vmem_limit_bytes=kib * 2**10),
            cost_estimate=pl.CostEstimate(flops=flops, bytes_accessed=2**20, transcendentals=0),
            name=name,
        )

    def slots(keys):
        return [pltpu.VMEM((keys, stack), F32), pltpu.VMEM((1, stack), F32)] * 2

    half = shape((BLOCK, 2 * width), BF16)
    pair, mid, coarse, inner, outer = call(
        project_pair,
        [shape((rows, 2 * width), BF16), shape((per_device, 2 * width), BF16), shape((blocks, 2 * width), BF16), half, half],
        [HBM] * 3,
        [VMEM] * 5,
        [pltpu.VMEM((rows, model), BF16), pltpu.VMEM((model, 2 * width), BF16), dma((2 + blocks,))],
        2 * 10**9,
        "pair",
        54000,
    )(tokens, w_key, w_value)

    state = [shape((KV_HEADS, blocks, stack, WIDE), BF16), shape((KV_HEADS, blocks, VROWS, stack), F32), shape((KV_HEADS, blocks, 1, stack), F32)]
    held = [pltpu.VMEM(part.shape, part.dtype) for part in state]
    spread = coarse
    level = GROUP
    while level < devices:
        spread = jnp.concatenate([spread, swap(spread, level)], axis=0)
        level *= 2
    spread = spread[blocks:]
    inner = swap(inner, 1)
    payload = jnp.pad(mid, ((0, spread.shape[0]), (0, 0)))
    payload = lax.optimization_barrier(jnp.broadcast_to(payload[None], (GROUP, *payload.shape)))
    links = [(i, i + 1) for i in range(1, devices - 1, 2)]
    outer = lax.ppermute(tied(outer, payload), "seq", links + [(b, a) for a, b in links])
    late = jnp.broadcast_to(spread[None], (GROUP, *spread.shape))
    payload = lax.dynamic_update_slice(payload, late, (0, per_device, 0))
    members = [list(range(at, at + GROUP)) for at in range(0, devices, GROUP)]
    arrived = lax.all_to_all(payload, "seq", 0, 0, axis_index_groups=members)

    q, acc, top = call(
        near,
        state,
        [VMEM, HBM, VMEM, VMEM, VMEM],
        [HBM] * 3,
        [pltpu.VMEM((KV_HEADS, model, SHARE * HEAD_DIM), BF16)]
        + held
        + [dma((2 * KV_HEADS + 1 + KV_HEADS * blocks,)), pltpu.VMEM((KV_HEADS, rows + 2 * BLOCK, WIDE), BF16), pltpu.VMEM((KV_HEADS, VROWS, rows + 2 * BLOCK), BF16)]
        + slots(rows + BLOCK),
        10**10,
        "near",
    )(tokens, w_query, tied(pair, payload), inner, outer)

    coarse_far = arrived[:, per_device:].reshape(-1, 2 * width)
    keys = (GROUP - 1) * per_device + coarse_far.shape[0]
    return call(
        far,
        shape((rows, w_out.shape[1]), BF16),
        [HBM] * 3 + [VMEM, VMEM, HBM],
        HBM,
        held
        + [
            pltpu.VMEM(w_out.shape, BF16),
            pltpu.VMEM((rows, w_out.shape[1]), BF16),
            dma((2 * KV_HEADS + 2 + blocks,)),
            pltpu.VMEM((keys, 2 * width), BF16),
            pltpu.VMEM((KV_HEADS, keys, WIDE), BF16),
            pltpu.VMEM((KV_HEADS, VROWS, keys), BF16),
            pltpu.VMEM((blocks, HEADS * HEAD_DIM, BLOCK), BF16),
        ]
        + slots(keys),
        8 * 10**9,
        "far",
    )(q, acc, top, arrived, coarse_far, w_out)


def solution(mesh):
    placed = (P("seq", None), P(), P(), P(), P())
    return jax.shard_map(body, mesh=mesh, in_specs=placed, out_specs=P("seq", None), check_vma=False)
```

```python
import math

import jax
import jax.numpy as jnp
from jax import lax
from jax.experimental import pallas as pl
from jax.experimental.pallas import tpu as pltpu
from jax.sharding import PartitionSpec as P

HEADS = 16
KV_HEADS = 4
HEAD_DIM = 64
BLOCK = 256
POOL = 16
GROUP = 16
SHARE = HEADS // KV_HEADS
WIDE = 128
VROWS = 80
BF16 = jnp.bfloat16
F32 = jnp.float32
NT = (((1,), (1,)), ((), ()))
TN = (((0,), (0,)), ((), ()))
MASKED = -1e30
VMEM = pl.BlockSpec(memory_space=pltpu.VMEM)
HBM = pl.BlockSpec(memory_space=pltpu.HBM)


def swap(rows, apart):
    count = lax.axis_size("seq")
    return lax.ppermute(rows, "seq", [(i, i ^ apart) for i in range(count)])


def tied(rows, *others):
    return lax.optimization_barrier((rows, *others))[0]


def project_pair(tokens_hbm, wk_hbm, wv_hbm, pair_ref, mid_ref, coarse_ref, inner_ref, outer_ref, tokens_ref, weight_ref, sems):
    rows = tokens_ref.shape[0]
    width = wk_hbm.shape[1]
    blocks = rows // BLOCK
    fetches = [pltpu.make_async_copy(wk_hbm, weight_ref.at[:, pl.ds(0, width)], sems.at[0])]
    fetches.append(pltpu.make_async_copy(wv_hbm, weight_ref.at[:, pl.ds(width, width)], sems.at[1]))
    for block in range(blocks):
        at = pl.ds(block * BLOCK, BLOCK)
        fetches.append(pltpu.make_async_copy(tokens_hbm.at[at], tokens_ref.at[at], sems.at[2 + block]))
    for fetch in fetches:
        fetch.start()
    even = lax.axis_index("seq") % 2 == 0
    runs = BLOCK // POOL
    tall = 3 * runs // 2
    row = lax.broadcasted_iota(jnp.int32, (tall, BLOCK), 0)
    column = lax.broadcasted_iota(jnp.int32, (tall, BLOCK), 1)
    share = jnp.where(row < runs, jnp.where(column // POOL == row, 1.0 / POOL, 0.0), jnp.where(row == runs, 1.0 / BLOCK, 0.0))
    share = share.astype(BF16)
    fetches[0].wait()
    fetches[1].wait()
    kept = []
    for block in range(blocks):
        at = slice(block * BLOCK, (block + 1) * BLOCK)
        fetches[2 + block].wait()
        held = jnp.dot(tokens_ref[at], weight_ref[...], preferred_element_type=F32).astype(BF16)
        pair_ref[at] = held
        kept.append(held)
        mean = jnp.dot(share, held, preferred_element_type=F32)
        mid_ref[block * runs : (block + 1) * runs] = mean[:runs].astype(BF16)
        coarse_ref[block : block + 1] = mean[runs : runs + 1].astype(BF16)
    inner_ref[...] = jnp.where(even, kept[-1], kept[0])
    outer_ref[...] = jnp.where(even, kept[0], kept[-1])


def put_keys(keys_ref, rows, at, biases):
    count = rows.shape[0]
    lane = lax.broadcasted_iota(jnp.int32, (count, HEAD_DIM), 1)
    extra = jnp.zeros((count, HEAD_DIM), F32)
    for order, bias in enumerate(biases):
        extra = jnp.where(lane == order, bias, extra)
    extra = extra.astype(BF16)
    for head in range(KV_HEADS):
        keys_ref[head, pl.ds(at, count), :HEAD_DIM] = rows[:, head * HEAD_DIM : (head + 1) * HEAD_DIM]
        keys_ref[head, pl.ds(at, count), HEAD_DIM:] = extra


def put_values(values_ref, rows):
    width = KV_HEADS * HEAD_DIM
    count = rows.shape[0]
    tall = KV_HEADS * VROWS
    row = lax.broadcasted_iota(jnp.int32, (tall, width), 0)
    column = lax.broadcasted_iota(jnp.int32, (tall, width), 1)
    head, inner = column // HEAD_DIM, column % HEAD_DIM
    pick = jnp.where(row == head * VROWS + inner, 1.0, 0.0).astype(BF16)
    turned = lax.dot_general(pick, rows, NT, preferred_element_type=F32)
    counting = lax.broadcasted_iota(jnp.int32, (tall, count), 0) % VROWS == HEAD_DIM
    values_ref[...] = jnp.where(counting, 1.0, turned).astype(BF16).reshape(KV_HEADS, VROWS, count)


def run_units(before, scores, finish, values, buffers, closing=None, between=None):
    def first(group, block):
        held, top = buffers[block]
        x, floor = scores(group, block)
        held[...] = x
        highest = jnp.max(x, axis=0, keepdims=True)
        top[...] = highest if floor is None else jnp.maximum(highest, floor)

    def second(group, block):
        held, top = buffers[block]
        highest = top[...]
        weights = jnp.exp(held[...] - highest).astype(BF16)
        finish(group, block, highest, jnp.dot(values(group, block), weights, preferred_element_type=F32))

    before(0)
    first(0, 0)

    def step(group, carry):
        before(group + 1)
        first(group, 1)
        second(group, 0)
        first(group + 1, 0)
        second(group, 1)
        return carry

    lax.fori_loop(0, KV_HEADS - 1, step, 0)
    if closing is not None:
        closing()
    last = KV_HEADS - 1
    first(last, 1)
    second(last, 0)
    if between is not None:
        between()
    second(last, 1)


def near(tokens_ref, wq_hbm, pair_ref, inner_ref, outer_ref, q_hbm, acc_hbm, top_hbm,
         wq_ref, q_ref, acc_ref, top_ref, sems, keys_ref, values_ref, sa, ta, sb, tb):
    rows = tokens_ref.shape[0]
    blocks = rows // BLOCK
    width = KV_HEADS * HEAD_DIM
    span = SHARE * HEAD_DIM
    me = lax.axis_index("seq")
    devices = lax.axis_size("seq")
    even = me % 2 == 0
    fetches = [
        pltpu.make_async_copy(wq_hbm.at[:, pl.ds(group * span, span)], wq_ref.at[group], sems.at[group])
        for group in range(KV_HEADS)
    ]
    for fetch in fetches:
        fetch.start()
    prev = jnp.where(even, outer_ref[...], inner_ref[...])
    follow = jnp.where(even, inner_ref[...], outer_ref[...])
    put_keys(keys_ref, prev[:, :width], 0, [jnp.where(me > 0, 0.0, MASKED)] * blocks)
    put_keys(keys_ref, pair_ref[:, :width], BLOCK, ())
    put_keys(keys_ref, follow[:, :width], BLOCK + rows, [jnp.where(me < devices - 1, 0.0, MASKED)] * blocks)
    put_values(values_ref, jnp.concatenate([prev[:, width:], pair_ref[:, width:], follow[:, width:]], axis=0))
    lane = lax.broadcasted_iota(jnp.int32, (BLOCK, HEAD_DIM), 1)

    def keep(group, source, target, order):
        return pltpu.make_async_copy(source.at[group], target.at[group], sems.at[order * KV_HEADS + group])

    def leave(group, block):
        return pltpu.make_async_copy(acc_ref.at[group, block], acc_hbm.at[group, block], sems.at[2 * KV_HEADS + 1 + group * blocks + block])

    def send(group):
        for block in range(blocks):
            leave(group, block).start()

    def before(group):
        pltpu.make_async_copy(wq_hbm.at[:, pl.ds(0, span)], wq_ref.at[group], sems.at[group]).wait()

        @pl.when(group >= 1)
        def _():
            keep(group - 1, q_ref, q_hbm, 1).start()

        @pl.when(group >= 2)
        def _():
            send(group - 2)

        part = jnp.dot(tokens_ref[...], wq_ref[group], preferred_element_type=F32)
        part = part.astype(BF16) * (1.0 / math.sqrt(HEAD_DIM))
        for block in range(blocks):
            extra = jnp.where(lane == block, 1.0, 0.0).astype(BF16)
            for head in range(SHARE):
                to = slice(head * BLOCK, (head + 1) * BLOCK)
                piece = part[block * BLOCK : (block + 1) * BLOCK, head * HEAD_DIM : (head + 1) * HEAD_DIM]
                q_ref[group, block, to, :HEAD_DIM] = piece
                q_ref[group, block, to, HEAD_DIM:] = extra

    def closing():
        keep(KV_HEADS - 1, q_ref, q_hbm, 1).start()
        send(KV_HEADS - 2)

    def scores(group, block):
        at = slice(block * BLOCK, block * BLOCK + BLOCK + rows)
        return lax.dot_general(keys_ref[group, at], q_ref[group, block], NT, preferred_element_type=F32), None

    def finish(group, block, highest, total):
        acc_ref[group, block] = total
        top_ref[group, block] = highest

    def values(group, block):
        return values_ref[group, :, block * BLOCK : block * BLOCK + BLOCK + rows]

    run_units(before, scores, finish, values, ((sa, ta), (sb, tb)), closing)
    send(KV_HEADS - 1)
    keep_top = pltpu.make_async_copy(top_ref, top_hbm, sems.at[2 * KV_HEADS])
    keep_top.start()
    for group in range(KV_HEADS):
        keep(group, q_ref, q_hbm, 1).wait()
        for block in range(blocks):
            leave(group, block).wait()
    keep_top.wait()


def far(q_hbm, acc_hbm, top_hbm, mids_ref, coarse_ref, wout_hbm, out_hbm,
        q_ref, acc_ref, top_ref, wout_ref, out_ref, sems, rows_ref, keys_ref, values_ref, mixed_ref, sa, ta, sb, tb):
    def fetch(group, source, target, order):
        return pltpu.make_async_copy(source.at[group], target.at[group], sems.at[order * KV_HEADS + group])

    fetch_top = pltpu.make_async_copy(top_hbm, top_ref, sems.at[2 * KV_HEADS])
    fetch_wout = pltpu.make_async_copy(wout_hbm, wout_ref, sems.at[2 * KV_HEADS + 1])
    fetch_top.start()
    for group in range(KV_HEADS):
        fetch(group, q_hbm, q_ref, 0).start()
        fetch(group, acc_hbm, acc_ref, 1).start()
    fetch_wout.start()
    blocks = mixed_ref.shape[0]
    width = KV_HEADS * HEAD_DIM
    me = lax.axis_index("seq")
    groups = lax.axis_size("seq") // GROUP
    mine = me % GROUP
    runs = BLOCK // POOL
    per_device = runs * blocks
    mid_rows = GROUP * per_device
    spread = blocks * (groups - 1)
    swapped = pl.multiple_of(mine * per_device, per_device)
    for member in range(GROUP):
        rows_ref[member * per_device : (member + 1) * per_device] = mids_ref[member, :per_device]
    rows_ref[pl.ds(swapped, per_device)] = coarse_ref[:per_device]
    if coarse_ref.shape[0] > per_device:
        rows_ref[mid_rows:] = coarse_ref[per_device:]
    indices = [me * blocks + block for block in range(blocks)]
    row = lax.broadcasted_iota(jnp.int32, (mid_rows, HEAD_DIM), 0)
    mid_block = (me - mine + row // per_device) * blocks + row % per_device // runs
    put_keys(keys_ref, rows_ref[:mid_rows, :width], 0, [jnp.where(jnp.abs(mid_block - index) > 1, 0.0, MASKED) for index in indices])
    for start in range(0, coarse_ref.shape[0], per_device):
        row = lax.broadcasted_iota(jnp.int32, (per_device, HEAD_DIM), 0) + start
        other = (row % spread) // blocks + 1
        far_block = (((me // GROUP) ^ other) * GROUP + row // spread) * blocks + row % blocks
        bias = [jnp.where(jnp.abs(far_block - index) > 1, 0.0, MASKED) for index in indices]
        at = swapped if start == 0 else mid_rows + start - per_device
        put_keys(keys_ref, coarse_ref[start : start + per_device, :width], at, bias)
    put_values(values_ref, rows_ref[:, width:])
    fetch_top.wait()

    def before(group):
        fetch(group, q_hbm, q_ref, 0).wait()
        fetch(group, acc_hbm, acc_ref, 1).wait()

    def scores(group, block):
        return lax.dot_general(keys_ref[group], q_ref[group, block], NT, preferred_element_type=F32), top_ref[group, block]

    def finish(group, block, highest, total):
        total = total + acc_ref[group, block] * jnp.exp(top_ref[group, block] - highest)
        share = total[:HEAD_DIM] / total[HEAD_DIM : HEAD_DIM + 1]
        share = share.astype(BF16)
        for head in range(SHARE):
            to = pl.multiple_of((group * SHARE + head) * HEAD_DIM, HEAD_DIM)
            mixed_ref[block, pl.ds(to, HEAD_DIM), :] = share[:, head * BLOCK : (head + 1) * BLOCK]

    def store(block):
        at = pl.ds(block * BLOCK, BLOCK)
        return pltpu.make_async_copy(out_ref.at[at], out_hbm.at[at], sems.at[2 * KV_HEADS + 2 + block])

    def project(block):
        at = pl.ds(block * BLOCK, BLOCK)
        out_ref[at] = lax.dot_general(mixed_ref[block], wout_ref[...], TN, preferred_element_type=F32).astype(BF16)

    run_units(before, scores, finish, lambda group, block: values_ref[group], ((sa, ta), (sb, tb)), fetch_wout.wait, lambda: project(0))
    store(0).start()
    for block in range(1, blocks):
        project(block)
        store(block).start()
    for block in range(blocks):
        store(block).wait()


def body(tokens, w_query, w_key, w_value, w_out):
    devices = lax.axis_size("seq")
    rows, model = tokens.shape
    blocks = rows // BLOCK
    width = KV_HEADS * HEAD_DIM
    stack = SHARE * BLOCK
    per_device = rows // POOL
    shape = jax.ShapeDtypeStruct
    dma = pltpu.SemaphoreType.DMA

    def call(kernel, out_shape, in_specs, out_specs, scratch, flops, name, kib=53000):
        return pl.pallas_call(
            kernel,
            out_shape=out_shape,
            in_specs=in_specs,
            out_specs=out_specs,
            scratch_shapes=scratch,
            compiler_params=pltpu.CompilerParams(vmem_limit_bytes=kib * 2**10),
            cost_estimate=pl.CostEstimate(flops=flops, bytes_accessed=2**20, transcendentals=0),
            name=name,
        )

    def slots(keys):
        return [pltpu.VMEM((keys, stack), F32), pltpu.VMEM((1, stack), F32)] * 2

    half = shape((BLOCK, 2 * width), BF16)
    pair, mid, coarse, inner, outer = call(
        project_pair,
        [shape((rows, 2 * width), BF16), shape((per_device, 2 * width), BF16), shape((blocks, 2 * width), BF16), half, half],
        [HBM] * 3,
        [VMEM] * 5,
        [pltpu.VMEM((rows, model), BF16), pltpu.VMEM((model, 2 * width), BF16), dma((2 + blocks,))],
        2 * 10**9,
        "pair",
        54000,
    )(tokens, w_key, w_value)

    state = [shape((KV_HEADS, blocks, stack, WIDE), BF16), shape((KV_HEADS, blocks, VROWS, stack), F32), shape((KV_HEADS, blocks, 1, stack), F32)]
    held = [pltpu.VMEM(part.shape, part.dtype) for part in state]
    spread = coarse
    level = GROUP
    while level < devices:
        spread = jnp.concatenate([spread, swap(spread, level)], axis=0)
        level *= 2
    spread = spread[blocks:]
    payload = jnp.pad(mid, ((0, spread.shape[0]), (0, 0)))
    payload = lax.optimization_barrier(jnp.broadcast_to(payload[None], (GROUP, *payload.shape)))
    links = [(i, i + 1) for i in range(1, devices - 1, 2)]
    outer = lax.ppermute(tied(outer, payload), "seq", links + [(b, a) for a, b in links])
    late = jnp.broadcast_to(spread[None], (GROUP, *spread.shape))
    payload = lax.dynamic_update_slice(payload, late, (0, per_device, 0))
    inner = swap(tied(inner, payload), 1)
    members = [list(range(at, at + GROUP)) for at in range(0, devices, GROUP)]
    arrived = lax.all_to_all(payload, "seq", 0, 0, axis_index_groups=members)

    q, acc, top = call(
        near,
        state,
        [VMEM, HBM, VMEM, VMEM, VMEM],
        [HBM] * 3,
        [pltpu.VMEM((KV_HEADS, model, SHARE * HEAD_DIM), BF16)]
        + held
        + [dma((2 * KV_HEADS + 1 + KV_HEADS * blocks,)), pltpu.VMEM((KV_HEADS, rows + 2 * BLOCK, WIDE), BF16), pltpu.VMEM((KV_HEADS, VROWS, rows + 2 * BLOCK), BF16)]
        + slots(rows + BLOCK),
        10**10,
        "near",
    )(tokens, w_query, tied(pair, payload), inner, outer)

    coarse_far = arrived[:, per_device:].reshape(-1, 2 * width)
    keys = (GROUP - 1) * per_device + coarse_far.shape[0]
    return call(
        far,
        shape((rows, w_out.shape[1]), BF16),
        [HBM] * 3 + [VMEM, VMEM, HBM],
        HBM,
        held
        + [
            pltpu.VMEM(w_out.shape, BF16),
            pltpu.VMEM((rows, w_out.shape[1]), BF16),
            dma((2 * KV_HEADS + 2 + blocks,)),
            pltpu.VMEM((keys, 2 * width), BF16),
            pltpu.VMEM((KV_HEADS, keys, WIDE), BF16),
            pltpu.VMEM((KV_HEADS, VROWS, keys), BF16),
            pltpu.VMEM((blocks, HEADS * HEAD_DIM, BLOCK), BF16),
        ]
        + slots(keys),
        8 * 10**9,
        "far",
    )(q, acc, top, arrived, coarse_far, w_out)


def solution(mesh):
    placed = (P("seq", None), P(), P(), P(), P())
    return jax.shard_map(body, mesh=mesh, in_specs=placed, out_specs=P("seq", None), check_vma=False)
```

```python
import math

import jax
import jax.numpy as jnp
from jax import lax
from jax.experimental import pallas as pl
from jax.experimental.pallas import tpu as pltpu
from jax.sharding import PartitionSpec as P

HEADS = 16
KV_HEADS = 4
HEAD_DIM = 64
BLOCK = 256
POOL = 16
GROUP = 16
SHARE = HEADS // KV_HEADS
WIDE = 128
VROWS = 80
BF16 = jnp.bfloat16
F32 = jnp.float32
NT = (((1,), (1,)), ((), ()))
TN = (((0,), (0,)), ((), ()))
MASKED = -1e30
VMEM = pl.BlockSpec(memory_space=pltpu.VMEM)
HBM = pl.BlockSpec(memory_space=pltpu.HBM)


def swap(rows, apart):
    count = lax.axis_size("seq")
    return lax.ppermute(rows, "seq", [(i, i ^ apart) for i in range(count)])


def tied(rows, *others):
    return lax.optimization_barrier((rows, *others))[0]


def project_pair(tokens_hbm, wk_hbm, wv_hbm, pair_ref, mid_ref, coarse_ref, inner_ref, outer_ref, tokens_ref, weight_ref, sems):
    rows = tokens_ref.shape[0]
    width = wk_hbm.shape[1]
    blocks = rows // BLOCK
    depth = tokens_ref.shape[1] // 2
    fetches = []
    for part in range(2):
        at = pl.ds(part * depth, depth)
        fetches.append(pltpu.make_async_copy(wk_hbm.at[at], weight_ref.at[at, pl.ds(0, width)], sems.at[3 * part]))
        fetches.append(pltpu.make_async_copy(wv_hbm.at[at], weight_ref.at[at, pl.ds(width, width)], sems.at[3 * part + 1]))
        fetches.append(pltpu.make_async_copy(tokens_hbm.at[:, at], tokens_ref.at[:, at], sems.at[3 * part + 2]))
    for fetch in fetches:
        fetch.start()
    even = lax.axis_index("seq") % 2 == 0
    runs = BLOCK // POOL
    tall = 3 * runs // 2
    row = lax.broadcasted_iota(jnp.int32, (tall, BLOCK), 0)
    column = lax.broadcasted_iota(jnp.int32, (tall, BLOCK), 1)
    share = jnp.where(row < runs, jnp.where(column // POOL == row, 1.0 / POOL, 0.0), jnp.where(row == runs, 1.0 / BLOCK, 0.0))
    share = share.astype(BF16)
    total = None
    for part in range(2):
        for fetch in fetches[3 * part : 3 * part + 3]:
            fetch.wait()
        at = slice(part * depth, (part + 1) * depth)
        product = jnp.dot(tokens_ref[:, at], weight_ref[at], preferred_element_type=F32)
        total = product if total is None else total + product
    kept = []
    for block in range(blocks):
        at = slice(block * BLOCK, (block + 1) * BLOCK)
        held = total[at].astype(BF16)
        pair_ref[at] = held
        kept.append(held)
        mean = jnp.dot(share, held, preferred_element_type=F32)
        mid_ref[block * runs : (block + 1) * runs] = mean[:runs].astype(BF16)
        coarse_ref[block : block + 1] = mean[runs : runs + 1].astype(BF16)
    inner_ref[...] = jnp.where(even, kept[-1], kept[0])
    outer_ref[...] = jnp.where(even, kept[0], kept[-1])


def put_keys(keys_ref, rows, at, biases):
    count = rows.shape[0]
    lane = lax.broadcasted_iota(jnp.int32, (count, HEAD_DIM), 1)
    extra = jnp.zeros((count, HEAD_DIM), F32)
    for order, bias in enumerate(biases):
        extra = jnp.where(lane == order, bias, extra)
    extra = extra.astype(BF16)
    for head in range(KV_HEADS):
        keys_ref[head, pl.ds(at, count), :HEAD_DIM] = rows[:, head * HEAD_DIM : (head + 1) * HEAD_DIM]
        keys_ref[head, pl.ds(at, count), HEAD_DIM:] = extra


def put_values(values_ref, rows):
    width = KV_HEADS * HEAD_DIM
    count = rows.shape[0]
    tall = KV_HEADS * VROWS
    row = lax.broadcasted_iota(jnp.int32, (tall, width), 0)
    column = lax.broadcasted_iota(jnp.int32, (tall, width), 1)
    head, inner = column // HEAD_DIM, column % HEAD_DIM
    pick = jnp.where(row == head * VROWS + inner, 1.0, 0.0).astype(BF16)
    turned = lax.dot_general(pick, rows, NT, preferred_element_type=F32)
    counting = lax.broadcasted_iota(jnp.int32, (tall, count), 0) % VROWS == HEAD_DIM
    values_ref[...] = jnp.where(counting, 1.0, turned).astype(BF16).reshape(KV_HEADS, VROWS, count)


def run_units(before, scores, finish, values, buffers, closing=None, between=None):
    def first(group, block):
        held, top = buffers[block]
        x, floor = scores(group, block)
        held[...] = x
        highest = jnp.max(x, axis=0, keepdims=True)
        top[...] = highest if floor is None else jnp.maximum(highest, floor)

    def second(group, block):
        held, top = buffers[block]
        highest = top[...]
        weights = jnp.exp(held[...] - highest).astype(BF16)
        finish(group, block, highest, jnp.dot(values(group, block), weights, preferred_element_type=F32))

    before(0)
    first(0, 0)

    def step(group, carry):
        before(group + 1)
        first(group, 1)
        second(group, 0)
        first(group + 1, 0)
        second(group, 1)
        return carry

    lax.fori_loop(0, KV_HEADS - 1, step, 0)
    if closing is not None:
        closing()
    last = KV_HEADS - 1
    first(last, 1)
    second(last, 0)
    if between is not None:
        between()
    second(last, 1)


def near(tokens_ref, wq_hbm, pair_ref, inner_ref, outer_ref, q_hbm, acc_hbm, top_hbm,
         wq_ref, q_ref, acc_ref, top_ref, sems, keys_ref, values_ref, sa, ta, sb, tb):
    rows = tokens_ref.shape[0]
    blocks = rows // BLOCK
    width = KV_HEADS * HEAD_DIM
    span = SHARE * HEAD_DIM
    me = lax.axis_index("seq")
    devices = lax.axis_size("seq")
    even = me % 2 == 0
    fetches = [
        pltpu.make_async_copy(wq_hbm.at[:, pl.ds(group * span, span)], wq_ref.at[group], sems.at[group])
        for group in range(KV_HEADS)
    ]
    for fetch in fetches:
        fetch.start()
    prev = jnp.where(even, outer_ref[...], inner_ref[...])
    follow = jnp.where(even, inner_ref[...], outer_ref[...])
    put_keys(keys_ref, prev[:, :width], 0, [jnp.where(me > 0, 0.0, MASKED)] * blocks)
    put_keys(keys_ref, pair_ref[:, :width], BLOCK, ())
    put_keys(keys_ref, follow[:, :width], BLOCK + rows, [jnp.where(me < devices - 1, 0.0, MASKED)] * blocks)
    put_values(values_ref, jnp.concatenate([prev[:, width:], pair_ref[:, width:], follow[:, width:]], axis=0))
    lane = lax.broadcasted_iota(jnp.int32, (BLOCK, HEAD_DIM), 1)

    def keep(group, source, target, order):
        return pltpu.make_async_copy(source.at[group], target.at[group], sems.at[order * KV_HEADS + group])

    def leave(group, block):
        return pltpu.make_async_copy(acc_ref.at[group, block], acc_hbm.at[group, block], sems.at[2 * KV_HEADS + 1 + group * blocks + block])

    def send(group):
        for block in range(blocks):
            leave(group, block).start()

    def before(group):
        pltpu.make_async_copy(wq_hbm.at[:, pl.ds(0, span)], wq_ref.at[group], sems.at[group]).wait()

        @pl.when(group >= 1)
        def _():
            keep(group - 1, q_ref, q_hbm, 1).start()

        @pl.when(group >= 2)
        def _():
            send(group - 2)

        part = jnp.dot(tokens_ref[...], wq_ref[group], preferred_element_type=F32)
        part = part.astype(BF16) * (1.0 / math.sqrt(HEAD_DIM))
        for block in range(blocks):
            extra = jnp.where(lane == block, 1.0, 0.0).astype(BF16)
            for head in range(SHARE):
                to = slice(head * BLOCK, (head + 1) * BLOCK)
                piece = part[block * BLOCK : (block + 1) * BLOCK, head * HEAD_DIM : (head + 1) * HEAD_DIM]
                q_ref[group, block, to, :HEAD_DIM] = piece
                q_ref[group, block, to, HEAD_DIM:] = extra

    def closing():
        keep(KV_HEADS - 1, q_ref, q_hbm, 1).start()
        send(KV_HEADS - 2)

    def scores(group, block):
        at = slice(block * BLOCK, block * BLOCK + BLOCK + rows)
        return lax.dot_general(keys_ref[group, at], q_ref[group, block], NT, preferred_element_type=F32), None

    def finish(group, block, highest, total):
        acc_ref[group, block] = total
        top_ref[group, block] = highest

    def values(group, block):
        return values_ref[group, :, block * BLOCK : block * BLOCK + BLOCK + rows]

    run_units(before, scores, finish, values, ((sa, ta), (sb, tb)), closing)
    send(KV_HEADS - 1)
    keep_top = pltpu.make_async_copy(top_ref, top_hbm, sems.at[2 * KV_HEADS])
    keep_top.start()
    for group in range(KV_HEADS):
        keep(group, q_ref, q_hbm, 1).wait()
        for block in range(blocks):
            leave(group, block).wait()
    keep_top.wait()


def far(q_hbm, acc_hbm, top_hbm, mids_ref, coarse_ref, wout_hbm, out_hbm,
        q_ref, acc_ref, top_ref, wout_ref, out_ref, sems, rows_ref, keys_ref, values_ref, mixed_ref, sa, ta, sb, tb):
    def fetch(group, source, target, order):
        return pltpu.make_async_copy(source.at[group], target.at[group], sems.at[order * KV_HEADS + group])

    fetch_top = pltpu.make_async_copy(top_hbm, top_ref, sems.at[2 * KV_HEADS])
    fetch_wout = pltpu.make_async_copy(wout_hbm, wout_ref, sems.at[2 * KV_HEADS + 1])
    fetch_top.start()
    for group in range(KV_HEADS):
        fetch(group, q_hbm, q_ref, 0).start()
        fetch(group, acc_hbm, acc_ref, 1).start()
    fetch_wout.start()
    blocks = mixed_ref.shape[0]
    width = KV_HEADS * HEAD_DIM
    me = lax.axis_index("seq")
    groups = lax.axis_size("seq") // GROUP
    mine = me % GROUP
    runs = BLOCK // POOL
    per_device = runs * blocks
    mid_rows = GROUP * per_device
    spread = blocks * (groups - 1)
    swapped = pl.multiple_of(mine * per_device, per_device)
    for member in range(GROUP):
        rows_ref[member * per_device : (member + 1) * per_device] = mids_ref[member, :per_device]
    rows_ref[pl.ds(swapped, per_device)] = coarse_ref[:per_device]
    if coarse_ref.shape[0] > per_device:
        rows_ref[mid_rows:] = coarse_ref[per_device:]
    indices = [me * blocks + block for block in range(blocks)]
    row = lax.broadcasted_iota(jnp.int32, (mid_rows, HEAD_DIM), 0)
    mid_block = (me - mine + row // per_device) * blocks + row % per_device // runs
    put_keys(keys_ref, rows_ref[:mid_rows, :width], 0, [jnp.where(jnp.abs(mid_block - index) > 1, 0.0, MASKED) for index in indices])
    for start in range(0, coarse_ref.shape[0], per_device):
        row = lax.broadcasted_iota(jnp.int32, (per_device, HEAD_DIM), 0) + start
        other = (row % spread) // blocks + 1
        far_block = (((me // GROUP) ^ other) * GROUP + row // spread) * blocks + row % blocks
        bias = [jnp.where(jnp.abs(far_block - index) > 1, 0.0, MASKED) for index in indices]
        at = swapped if start == 0 else mid_rows + start - per_device
        put_keys(keys_ref, coarse_ref[start : start + per_device, :width], at, bias)
    put_values(values_ref, rows_ref[:, width:])
    fetch_top.wait()

    def before(group):
        fetch(group, q_hbm, q_ref, 0).wait()
        fetch(group, acc_hbm, acc_ref, 1).wait()

    def scores(group, block):
        return lax.dot_general(keys_ref[group], q_ref[group, block], NT, preferred_element_type=F32), top_ref[group, block]

    def finish(group, block, highest, total):
        total = total + acc_ref[group, block] * jnp.exp(top_ref[group, block] - highest)
        share = total[:HEAD_DIM] / total[HEAD_DIM : HEAD_DIM + 1]
        share = share.astype(BF16)
        for head in range(SHARE):
            to = pl.multiple_of((group * SHARE + head) * HEAD_DIM, HEAD_DIM)
            mixed_ref[block, pl.ds(to, HEAD_DIM), :] = share[:, head * BLOCK : (head + 1) * BLOCK]

    def store(block):
        at = pl.ds(block * BLOCK, BLOCK)
        return pltpu.make_async_copy(out_ref.at[at], out_hbm.at[at], sems.at[2 * KV_HEADS + 2 + block])

    def project(block):
        at = pl.ds(block * BLOCK, BLOCK)
        out_ref[at] = lax.dot_general(mixed_ref[block], wout_ref[...], TN, preferred_element_type=F32).astype(BF16)

    run_units(before, scores, finish, lambda group, block: values_ref[group], ((sa, ta), (sb, tb)), fetch_wout.wait, lambda: project(0))
    store(0).start()
    for block in range(1, blocks):
        project(block)
        store(block).start()
    for block in range(blocks):
        store(block).wait()


def body(tokens, w_query, w_key, w_value, w_out):
    devices = lax.axis_size("seq")
    rows, model = tokens.shape
    blocks = rows // BLOCK
    width = KV_HEADS * HEAD_DIM
    stack = SHARE * BLOCK
    per_device = rows // POOL
    shape = jax.ShapeDtypeStruct
    dma = pltpu.SemaphoreType.DMA

    def call(kernel, out_shape, in_specs, out_specs, scratch, flops, name, kib=53000):
        return pl.pallas_call(
            kernel,
            out_shape=out_shape,
            in_specs=in_specs,
            out_specs=out_specs,
            scratch_shapes=scratch,
            compiler_params=pltpu.CompilerParams(vmem_limit_bytes=kib * 2**10),
            cost_estimate=pl.CostEstimate(flops=flops, bytes_accessed=2**20, transcendentals=0),
            name=name,
        )

    def slots(keys):
        return [pltpu.VMEM((keys, stack), F32), pltpu.VMEM((1, stack), F32)] * 2

    half = shape((BLOCK, 2 * width), BF16)
    pair, mid, coarse, inner, outer = call(
        project_pair,
        [shape((rows, 2 * width), BF16), shape((per_device, 2 * width), BF16), shape((blocks, 2 * width), BF16), half, half],
        [HBM] * 3,
        [VMEM] * 5,
        [pltpu.VMEM((rows, model), BF16), pltpu.VMEM((model, 2 * width), BF16), dma((6,))],
        2 * 10**9,
        "pair",
        54000,
    )(tokens, w_key, w_value)

    state = [shape((KV_HEADS, blocks, stack, WIDE), BF16), shape((KV_HEADS, blocks, VROWS, stack), F32), shape((KV_HEADS, blocks, 1, stack), F32)]
    held = [pltpu.VMEM(part.shape, part.dtype) for part in state]
    spread = coarse
    level = GROUP
    while level < devices:
        spread = jnp.concatenate([spread, swap(spread, level)], axis=0)
        level *= 2
    spread = spread[blocks:]
    payload = jnp.pad(mid, ((0, spread.shape[0]), (0, 0)))
    payload = lax.optimization_barrier(jnp.broadcast_to(payload[None], (GROUP, *payload.shape)))
    links = [(i, i + 1) for i in range(1, devices - 1, 2)]
    outer = lax.ppermute(tied(outer, payload), "seq", links + [(b, a) for a, b in links])
    late = jnp.broadcast_to(spread[None], (GROUP, *spread.shape))
    payload = lax.dynamic_update_slice(payload, late, (0, per_device, 0))
    inner = swap(tied(inner, payload), 1)
    members = [list(range(at, at + GROUP)) for at in range(0, devices, GROUP)]
    arrived = lax.all_to_all(payload, "seq", 0, 0, axis_index_groups=members)

    q, acc, top = call(
        near,
        state,
        [VMEM, HBM, VMEM, VMEM, VMEM],
        [HBM] * 3,
        [pltpu.VMEM((KV_HEADS, model, SHARE * HEAD_DIM), BF16)]
        + held
        + [dma((2 * KV_HEADS + 1 + KV_HEADS * blocks,)), pltpu.VMEM((KV_HEADS, rows + 2 * BLOCK, WIDE), BF16), pltpu.VMEM((KV_HEADS, VROWS, rows + 2 * BLOCK), BF16)]
        + slots(rows + BLOCK),
        10**10,
        "near",
    )(tokens, w_query, tied(pair, payload), inner, outer)

    coarse_far = arrived[:, per_device:].reshape(-1, 2 * width)
    keys = (GROUP - 1) * per_device + coarse_far.shape[0]
    return call(
        far,
        shape((rows, w_out.shape[1]), BF16),
        [HBM] * 3 + [VMEM, VMEM, HBM],
        HBM,
        held
        + [
            pltpu.VMEM(w_out.shape, BF16),
            pltpu.VMEM((rows, w_out.shape[1]), BF16),
            dma((2 * KV_HEADS + 2 + blocks,)),
            pltpu.VMEM((keys, 2 * width), BF16),
            pltpu.VMEM((KV_HEADS, keys, WIDE), BF16),
            pltpu.VMEM((KV_HEADS, VROWS, keys), BF16),
            pltpu.VMEM((blocks, HEADS * HEAD_DIM, BLOCK), BF16),
        ]
        + slots(keys),
        8 * 10**9,
        "far",
    )(q, acc, top, arrived, coarse_far, w_out)


def solution(mesh):
    placed = (P("seq", None), P(), P(), P(), P())
    return jax.shard_map(body, mesh=mesh, in_specs=placed, out_specs=P("seq", None), check_vma=False)
```

```python
import math

import jax
import jax.numpy as jnp
from jax import lax
from jax.experimental import pallas as pl
from jax.experimental.pallas import tpu as pltpu
from jax.sharding import PartitionSpec as P

HEADS = 16
KV_HEADS = 4
HEAD_DIM = 64
BLOCK = 256
POOL = 16
GROUP = 16
SHARE = HEADS // KV_HEADS
WIDE = 128
VROWS = 80
BF16 = jnp.bfloat16
F32 = jnp.float32
NT = (((1,), (1,)), ((), ()))
TN = (((0,), (0,)), ((), ()))
MASKED = -1e30
VMEM = pl.BlockSpec(memory_space=pltpu.VMEM)
HBM = pl.BlockSpec(memory_space=pltpu.HBM)


def swap(rows, apart):
    count = lax.axis_size("seq")
    return lax.ppermute(rows, "seq", [(i, i ^ apart) for i in range(count)])


def tied(rows, *others):
    return lax.optimization_barrier((rows, *others))[0]


def project_pair(tokens_hbm, wk_hbm, wv_hbm, pair_ref, mid_ref, coarse_ref, inner_ref, outer_ref, tokens_ref, weight_ref, sems):
    rows = tokens_ref.shape[0]
    width = wk_hbm.shape[1]
    blocks = rows // BLOCK
    depth = tokens_ref.shape[1] // 4
    fetches = []
    for part in range(4):
        at = pl.ds(part * depth, depth)
        fetches.append(pltpu.make_async_copy(wk_hbm.at[at], weight_ref.at[at, pl.ds(0, width)], sems.at[3 * part]))
        fetches.append(pltpu.make_async_copy(wv_hbm.at[at], weight_ref.at[at, pl.ds(width, width)], sems.at[3 * part + 1]))
        fetches.append(pltpu.make_async_copy(tokens_hbm.at[:, at], tokens_ref.at[:, at], sems.at[3 * part + 2]))
    for fetch in fetches:
        fetch.start()
    even = lax.axis_index("seq") % 2 == 0
    runs = BLOCK // POOL
    tall = 3 * runs // 2
    row = lax.broadcasted_iota(jnp.int32, (tall, BLOCK), 0)
    column = lax.broadcasted_iota(jnp.int32, (tall, BLOCK), 1)
    share = jnp.where(row < runs, jnp.where(column // POOL == row, 1.0 / POOL, 0.0), jnp.where(row == runs, 1.0 / BLOCK, 0.0))
    share = share.astype(BF16)
    total = None
    for part in range(4):
        for fetch in fetches[3 * part : 3 * part + 3]:
            fetch.wait()
        at = slice(part * depth, (part + 1) * depth)
        product = jnp.dot(tokens_ref[:, at], weight_ref[at], preferred_element_type=F32)
        total = product if total is None else total + product
    kept = []
    for block in range(blocks):
        at = slice(block * BLOCK, (block + 1) * BLOCK)
        held = total[at].astype(BF16)
        pair_ref[at] = held
        kept.append(held)
        mean = jnp.dot(share, held, preferred_element_type=F32)
        mid_ref[block * runs : (block + 1) * runs] = mean[:runs].astype(BF16)
        coarse_ref[block : block + 1] = mean[runs : runs + 1].astype(BF16)
    inner_ref[...] = jnp.where(even, kept[-1], kept[0])
    outer_ref[...] = jnp.where(even, kept[0], kept[-1])


def put_keys(keys_ref, rows, at, biases):
    count = rows.shape[0]
    lane = lax.broadcasted_iota(jnp.int32, (count, HEAD_DIM), 1)
    extra = jnp.zeros((count, HEAD_DIM), F32)
    for order, bias in enumerate(biases):
        extra = jnp.where(lane == order, bias, extra)
    extra = extra.astype(BF16)
    for head in range(KV_HEADS):
        keys_ref[head, pl.ds(at, count), :HEAD_DIM] = rows[:, head * HEAD_DIM : (head + 1) * HEAD_DIM]
        keys_ref[head, pl.ds(at, count), HEAD_DIM:] = extra


def put_values(values_ref, rows):
    width = KV_HEADS * HEAD_DIM
    count = rows.shape[0]
    tall = KV_HEADS * VROWS
    row = lax.broadcasted_iota(jnp.int32, (tall, width), 0)
    column = lax.broadcasted_iota(jnp.int32, (tall, width), 1)
    head, inner = column // HEAD_DIM, column % HEAD_DIM
    pick = jnp.where(row == head * VROWS + inner, 1.0, 0.0).astype(BF16)
    turned = lax.dot_general(pick, rows, NT, preferred_element_type=F32)
    counting = lax.broadcasted_iota(jnp.int32, (tall, count), 0) % VROWS == HEAD_DIM
    values_ref[...] = jnp.where(counting, 1.0, turned).astype(BF16).reshape(KV_HEADS, VROWS, count)


def run_units(before, scores, finish, values, buffers, closing=None, between=None):
    def first(group, block):
        held, top = buffers[block]
        x, floor = scores(group, block)
        held[...] = x
        highest = jnp.max(x, axis=0, keepdims=True)
        top[...] = highest if floor is None else jnp.maximum(highest, floor)

    def second(group, block):
        held, top = buffers[block]
        highest = top[...]
        weights = jnp.exp(held[...] - highest).astype(BF16)
        finish(group, block, highest, jnp.dot(values(group, block), weights, preferred_element_type=F32))

    before(0)
    first(0, 0)

    def step(group, carry):
        before(group + 1)
        first(group, 1)
        second(group, 0)
        first(group + 1, 0)
        second(group, 1)
        return carry

    lax.fori_loop(0, KV_HEADS - 1, step, 0)
    if closing is not None:
        closing()
    last = KV_HEADS - 1
    first(last, 1)
    second(last, 0)
    if between is not None:
        between()
    second(last, 1)


def near(tokens_ref, wq_hbm, pair_ref, inner_ref, outer_ref, q_hbm, acc_hbm, top_hbm,
         wq_ref, q_ref, acc_ref, top_ref, sems, keys_ref, values_ref, sa, ta, sb, tb):
    rows = tokens_ref.shape[0]
    blocks = rows // BLOCK
    width = KV_HEADS * HEAD_DIM
    span = SHARE * HEAD_DIM
    me = lax.axis_index("seq")
    devices = lax.axis_size("seq")
    even = me % 2 == 0
    fetches = [
        pltpu.make_async_copy(wq_hbm.at[:, pl.ds(group * span, span)], wq_ref.at[group], sems.at[group])
        for group in range(KV_HEADS)
    ]
    for fetch in fetches:
        fetch.start()
    prev = jnp.where(even, outer_ref[...], inner_ref[...])
    follow = jnp.where(even, inner_ref[...], outer_ref[...])
    put_keys(keys_ref, prev[:, :width], 0, [jnp.where(me > 0, 0.0, MASKED)] * blocks)
    put_keys(keys_ref, pair_ref[:, :width], BLOCK, ())
    put_keys(keys_ref, follow[:, :width], BLOCK + rows, [jnp.where(me < devices - 1, 0.0, MASKED)] * blocks)
    put_values(values_ref, jnp.concatenate([prev[:, width:], pair_ref[:, width:], follow[:, width:]], axis=0))
    lane = lax.broadcasted_iota(jnp.int32, (BLOCK, HEAD_DIM), 1)

    def keep(group, source, target, order):
        return pltpu.make_async_copy(source.at[group], target.at[group], sems.at[order * KV_HEADS + group])

    def leave(group, block):
        return pltpu.make_async_copy(acc_ref.at[group, block], acc_hbm.at[group, block], sems.at[2 * KV_HEADS + 1 + group * blocks + block])

    def send(group):
        for block in range(blocks):
            leave(group, block).start()

    def before(group):
        pltpu.make_async_copy(wq_hbm.at[:, pl.ds(0, span)], wq_ref.at[group], sems.at[group]).wait()

        @pl.when(group >= 1)
        def _():
            keep(group - 1, q_ref, q_hbm, 1).start()

        @pl.when(group >= 2)
        def _():
            send(group - 2)

        part = jnp.dot(tokens_ref[...], wq_ref[group], preferred_element_type=F32)
        part = part.astype(BF16) * (1.0 / math.sqrt(HEAD_DIM))
        for block in range(blocks):
            extra = jnp.where(lane == block, 1.0, 0.0).astype(BF16)
            for head in range(SHARE):
                to = slice(head * BLOCK, (head + 1) * BLOCK)
                piece = part[block * BLOCK : (block + 1) * BLOCK, head * HEAD_DIM : (head + 1) * HEAD_DIM]
                q_ref[group, block, to, :HEAD_DIM] = piece
                q_ref[group, block, to, HEAD_DIM:] = extra

    def closing():
        keep(KV_HEADS - 1, q_ref, q_hbm, 1).start()
        send(KV_HEADS - 2)

    def scores(group, block):
        at = slice(block * BLOCK, block * BLOCK + BLOCK + rows)
        return lax.dot_general(keys_ref[group, at], q_ref[group, block], NT, preferred_element_type=F32), None

    def finish(group, block, highest, total):
        acc_ref[group, block] = total
        top_ref[group, block] = highest

    def values(group, block):
        return values_ref[group, :, block * BLOCK : block * BLOCK + BLOCK + rows]

    run_units(before, scores, finish, values, ((sa, ta), (sb, tb)), closing)
    send(KV_HEADS - 1)
    keep_top = pltpu.make_async_copy(top_ref, top_hbm, sems.at[2 * KV_HEADS])
    keep_top.start()
    for group in range(KV_HEADS):
        keep(group, q_ref, q_hbm, 1).wait()
        for block in range(blocks):
            leave(group, block).wait()
    keep_top.wait()


def far(q_hbm, acc_hbm, top_hbm, mids_ref, coarse_ref, wout_hbm, out_hbm,
        q_ref, acc_ref, top_ref, wout_ref, out_ref, sems, rows_ref, keys_ref, values_ref, mixed_ref, sa, ta, sb, tb):
    def fetch(group, source, target, order):
        return pltpu.make_async_copy(source.at[group], target.at[group], sems.at[order * KV_HEADS + group])

    fetch_top = pltpu.make_async_copy(top_hbm, top_ref, sems.at[2 * KV_HEADS])
    fetch_wout = pltpu.make_async_copy(wout_hbm, wout_ref, sems.at[2 * KV_HEADS + 1])
    fetch_top.start()
    for group in range(KV_HEADS):
        fetch(group, q_hbm, q_ref, 0).start()
        fetch(group, acc_hbm, acc_ref, 1).start()
    fetch_wout.start()
    blocks = mixed_ref.shape[0]
    width = KV_HEADS * HEAD_DIM
    me = lax.axis_index("seq")
    groups = lax.axis_size("seq") // GROUP
    mine = me % GROUP
    runs = BLOCK // POOL
    per_device = runs * blocks
    mid_rows = GROUP * per_device
    spread = blocks * (groups - 1)
    swapped = pl.multiple_of(mine * per_device, per_device)
    for member in range(GROUP):
        rows_ref[member * per_device : (member + 1) * per_device] = mids_ref[member, :per_device]
    rows_ref[pl.ds(swapped, per_device)] = coarse_ref[:per_device]
    if coarse_ref.shape[0] > per_device:
        rows_ref[mid_rows:] = coarse_ref[per_device:]
    indices = [me * blocks + block for block in range(blocks)]
    row = lax.broadcasted_iota(jnp.int32, (mid_rows, HEAD_DIM), 0)
    mid_block = (me - mine + row // per_device) * blocks + row % per_device // runs
    put_keys(keys_ref, rows_ref[:mid_rows, :width], 0, [jnp.where(jnp.abs(mid_block - index) > 1, 0.0, MASKED) for index in indices])
    for start in range(0, coarse_ref.shape[0], per_device):
        row = lax.broadcasted_iota(jnp.int32, (per_device, HEAD_DIM), 0) + start
        other = (row % spread) // blocks + 1
        far_block = (((me // GROUP) ^ other) * GROUP + row // spread) * blocks + row % blocks
        bias = [jnp.where(jnp.abs(far_block - index) > 1, 0.0, MASKED) for index in indices]
        at = swapped if start == 0 else mid_rows + start - per_device
        put_keys(keys_ref, coarse_ref[start : start + per_device, :width], at, bias)
    put_values(values_ref, rows_ref[:, width:])
    fetch_top.wait()

    def before(group):
        fetch(group, q_hbm, q_ref, 0).wait()
        fetch(group, acc_hbm, acc_ref, 1).wait()

    def scores(group, block):
        return lax.dot_general(keys_ref[group], q_ref[group, block], NT, preferred_element_type=F32), top_ref[group, block]

    def finish(group, block, highest, total):
        total = total + acc_ref[group, block] * jnp.exp(top_ref[group, block] - highest)
        share = total[:HEAD_DIM] / total[HEAD_DIM : HEAD_DIM + 1]
        share = share.astype(BF16)
        for head in range(SHARE):
            to = pl.multiple_of((group * SHARE + head) * HEAD_DIM, HEAD_DIM)
            mixed_ref[block, pl.ds(to, HEAD_DIM), :] = share[:, head * BLOCK : (head + 1) * BLOCK]

    def store(block):
        at = pl.ds(block * BLOCK, BLOCK)
        return pltpu.make_async_copy(out_ref.at[at], out_hbm.at[at], sems.at[2 * KV_HEADS + 2 + block])

    def project(block):
        at = pl.ds(block * BLOCK, BLOCK)
        out_ref[at] = lax.dot_general(mixed_ref[block], wout_ref[...], TN, preferred_element_type=F32).astype(BF16)

    run_units(before, scores, finish, lambda group, block: values_ref[group], ((sa, ta), (sb, tb)), fetch_wout.wait, lambda: project(0))
    store(0).start()
    for block in range(1, blocks):
        project(block)
        store(block).start()
    for block in range(blocks):
        store(block).wait()


def body(tokens, w_query, w_key, w_value, w_out):
    devices = lax.axis_size("seq")
    rows, model = tokens.shape
    blocks = rows // BLOCK
    width = KV_HEADS * HEAD_DIM
    stack = SHARE * BLOCK
    per_device = rows // POOL
    shape = jax.ShapeDtypeStruct
    dma = pltpu.SemaphoreType.DMA

    def call(kernel, out_shape, in_specs, out_specs, scratch, flops, name, kib=53000):
        return pl.pallas_call(
            kernel,
            out_shape=out_shape,
            in_specs=in_specs,
            out_specs=out_specs,
            scratch_shapes=scratch,
            compiler_params=pltpu.CompilerParams(vmem_limit_bytes=kib * 2**10),
            cost_estimate=pl.CostEstimate(flops=flops, bytes_accessed=2**20, transcendentals=0),
            name=name,
        )

    def slots(keys):
        return [pltpu.VMEM((keys, stack), F32), pltpu.VMEM((1, stack), F32)] * 2

    half = shape((BLOCK, 2 * width), BF16)
    pair, mid, coarse, inner, outer = call(
        project_pair,
        [shape((rows, 2 * width), BF16), shape((per_device, 2 * width), BF16), shape((blocks, 2 * width), BF16), half, half],
        [HBM] * 3,
        [VMEM] * 5,
        [pltpu.VMEM((rows, model), BF16), pltpu.VMEM((model, 2 * width), BF16), dma((12,))],
        2 * 10**9,
        "pair",
        54000,
    )(tokens, w_key, w_value)

    state = [shape((KV_HEADS, blocks, stack, WIDE), BF16), shape((KV_HEADS, blocks, VROWS, stack), F32), shape((KV_HEADS, blocks, 1, stack), F32)]
    held = [pltpu.VMEM(part.shape, part.dtype) for part in state]
    spread = coarse
    level = GROUP
    while level < devices:
        spread = jnp.concatenate([spread, swap(spread, level)], axis=0)
        level *= 2
    spread = spread[blocks:]
    payload = jnp.pad(mid, ((0, spread.shape[0]), (0, 0)))
    payload = lax.optimization_barrier(jnp.broadcast_to(payload[None], (GROUP, *payload.shape)))
    links = [(i, i + 1) for i in range(1, devices - 1, 2)]
    outer = lax.ppermute(tied(outer, payload), "seq", links + [(b, a) for a, b in links])
    late = jnp.broadcast_to(spread[None], (GROUP, *spread.shape))
    payload = lax.dynamic_update_slice(payload, late, (0, per_device, 0))
    inner = swap(tied(inner, payload), 1)
    members = [list(range(at, at + GROUP)) for at in range(0, devices, GROUP)]
    arrived = lax.all_to_all(payload, "seq", 0, 0, axis_index_groups=members)

    q, acc, top = call(
        near,
        state,
        [VMEM, HBM, VMEM, VMEM, VMEM],
        [HBM] * 3,
        [pltpu.VMEM((KV_HEADS, model, SHARE * HEAD_DIM), BF16)]
        + held
        + [dma((2 * KV_HEADS + 1 + KV_HEADS * blocks,)), pltpu.VMEM((KV_HEADS, rows + 2 * BLOCK, WIDE), BF16), pltpu.VMEM((KV_HEADS, VROWS, rows + 2 * BLOCK), BF16)]
        + slots(rows + BLOCK),
        10**10,
        "near",
    )(tokens, w_query, tied(pair, payload), inner, outer)

    coarse_far = arrived[:, per_device:].reshape(-1, 2 * width)
    keys = (GROUP - 1) * per_device + coarse_far.shape[0]
    return call(
        far,
        shape((rows, w_out.shape[1]), BF16),
        [HBM] * 3 + [VMEM, VMEM, HBM],
        HBM,
        held
        + [
            pltpu.VMEM(w_out.shape, BF16),
            pltpu.VMEM((rows, w_out.shape[1]), BF16),
            dma((2 * KV_HEADS + 2 + blocks,)),
            pltpu.VMEM((keys, 2 * width), BF16),
            pltpu.VMEM((KV_HEADS, keys, WIDE), BF16),
            pltpu.VMEM((KV_HEADS, VROWS, keys), BF16),
            pltpu.VMEM((blocks, HEADS * HEAD_DIM, BLOCK), BF16),
        ]
        + slots(keys),
        8 * 10**9,
        "far",
    )(q, acc, top, arrived, coarse_far, w_out)


def solution(mesh):
    placed = (P("seq", None), P(), P(), P(), P())
    return jax.shard_map(body, mesh=mesh, in_specs=placed, out_specs=P("seq", None), check_vma=False)
```
